32 devices in a mesh: groups: 2 (over x), tower: 2 (over core), inner: 8 (over z, y).
Axes of the slice: x: 2, y: 2, z: 4, core: 2. Of those that a mesh axis runs over, the one named last changes fastest.
Arguments:
- ids: int32 [2, 64, 2048, 4], P('tower', 'inner', 'groups'), parts along dimension 2, may hold values from 0 to 16383
- bag_len: int32 [2, 64, 2048], P('tower', 'inner', 'groups'), parts along dimension 2, may hold values from 1 to 4
- slot_of_feature: int32 [2, 64], P('tower'), may hold values from 0 to 63, each once within a row
- tables: bfloat16 [2, 64, 16384, 24], P('tower', 'inner'), may hold values from -3 to 3
- cross_w: bfloat16 [2, 1536, 1536], P('tower'), may hold values from -0.15625 to 0.15625
- cross_b: float32 [2, 1536], P('tower'), may hold values from -3 to 3
- comp_w: bfloat16 [2, 1536, 64], P('tower'), may hold values from -0.15625 to 0.15625
- comp_b: float32 [2, 64], P('tower'), may hold values from -3 to 3
- other_towers: bfloat16 [2048, 896], P(('groups', 'inner')), parts along dimension 0, may hold values from -6 to 6
- expert_w: bfloat16 [8, 1024, 512], P('tower'), may hold values from -0.1875 to 0.1875
- expert_b: float32 [8, 512], P('tower'), may hold values from -3 to 3
- gate_w: bfloat16 [1024, 4, 8], replicated, may hold values from -0.1875 to 0.1875
Outputs:
- task_mix: bfloat16 [2048, 4, 512], P(('groups', 'inner'), None, 'tower'), parts along dimension 0
The draws below stay inside these ranges and needn't reach their ends.
There are 2 independent parts, one for each index of `groups`. The reference program is written for one: setup_inputs(seed, part) draws one part's arguments, and reference() takes and returns one part's arrays. A program takes and returns all parts, laid end to end along the dimension named above; an argument that names none is the same for every part. Nothing has to cross between parts.
Inputs may be any that keep to these rules, and one draw needn't show every extreme that they name: `bag_len`: every bag holds at least one id. `slot_of_feature`: each row is a permutation of the 64 slots.
All inputs are finite; a program needn't handle non-finite values.
Results may differ from the reference program's by a relative error of at most 0.0095.
Values may be sent and summed in bfloat16 or wider, within the bound.
No kernel may reach another device: no remote copies, remote signals or barrier semaphores. Data moves between devices by JAX's collectives and lax.ppermute only.
A program may use at most 128 MiB of HBM per device.

```python
import math
import jax
import jax.numpy as jnp
import numpy as np
from jax import lax

WIDTH = 1536
NF = 64
ED = 24
VOCAB = 16384
BAG = 4
CW = 64
EIN = 1024
HID = 512
TASKS = 4
TOWERS = 2
EXPERTS = 8
OTHER = 896
SAMPLES = 1024


def with_ends(result, key, low, high):
    longest = result.shape.index(max(result.shape))
    spots = []
    for shift in (0, 1):
        where = [jax.random.randint(jax.random.fold_in(key, axis), (), 0, length) for axis, length in enumerate(result.shape)]
        where[longest] = (where[longest] + shift) % result.shape[longest]
        spots.append(tuple(where))
    return result.at[spots[0]].set(low).at[spots[1]].set(high)


def levels(rng, shape, pieces, least, high):
    factor_of, own = 1.0, jax.random.fold_in(rng, 6)
    for axis_at, blocks in pieces:
        draws = jnp.exp(jax.random.uniform(jax.random.fold_in(own, axis_at), (blocks,), jnp.float32, least / len(pieces), high / len(pieces)))
        factor_of = factor_of * jnp.repeat(draws, shape[axis_at] // blocks).reshape([-1 if axis == axis_at else 1 for axis in range(len(shape))])
    return factor_of


def cumulative_ranks(amount, slope):
    loads = [(1 << 20) // math.isqrt(standing ** slope) + 1 for standing in range(1, amount + 1)]
    scale = 1 + sum(loads) // (1 << 30)
    return np.cumsum(np.array([max(1, weight // scale) for weight in loads]))


def ranked(rng, shape, amount, lean):
    grid = cumulative_ranks(amount, lean)
    lot = jax.random.randint(jax.random.fold_in(rng, 1), shape, 0, int(grid[amount - 1]))
    standing = jnp.searchsorted(jnp.asarray(grid, jnp.int32), lot, side="right")
    return jax.random.permutation(jax.random.fold_in(rng, 2), amount)[standing].astype(jnp.int32)


def centred(own_key, dims, spread, bound, split=(), dtype=jnp.bfloat16):
    gain = levels(own_key, dims, split, -0.22, 0.18) if split else 1.0
    values = jax.random.normal(own_key, dims, jnp.float32) * spread * gain
    return jnp.minimum(jnp.maximum(values, -bound), bound).astype(dtype)


def setup_inputs(seed: int = 0, part: int = 0) -> dict:
    streams_of = jax.random.split(jax.random.key(seed), 13)
    part_splits = jax.random.split(jax.random.fold_in(streams_of[12], part), 13)
    ids = with_ends(ranked(part_splits[0], (TOWERS, NF, SAMPLES, BAG), VOCAB, 2), jax.random.fold_in(part_splits[0], 3), 0, VOCAB - 1).astype(jnp.int32)
    bag_len = with_ends(jax.random.randint(part_splits[1], (TOWERS, NF, SAMPLES), 1, BAG + 1), jax.random.fold_in(part_splits[1], 1), 1, BAG).astype(jnp.int32)
    slot_of_feature = jax.vmap(lambda own: jax.random.permutation(own, NF))(jax.random.split(streams_of[2], TOWERS)).reshape((TOWERS, NF)).astype(jnp.int32)
    tables = centred(streams_of[3], (TOWERS, NF, VOCAB, ED), 0.5, 3.0, ((0, 2), (1, 8)))
    cross_w = centred(streams_of[4], (TOWERS, WIDTH, WIDTH), WIDTH ** -0.5, 0.15625, ((0, 2),))
    cross_b = centred(streams_of[5], (TOWERS, WIDTH), 0.5, 3.0, ((0, 2),), jnp.float32)
    comp_w = centred(streams_of[6], (TOWERS, WIDTH, CW), WIDTH ** -0.5, 0.15625, ((0, 2),))
    comp_b = centred(streams_of[7], (TOWERS, CW), 0.5, 3.0, ((0, 2),), jnp.float32)
    other_towers = centred(part_splits[8], (SAMPLES, OTHER), 1.0, 6.0, ((0, 8),))
    expert_w = centred(streams_of[9], (EXPERTS, EIN, HID), EIN ** -0.5, 0.1875, ((0, 2),))
    expert_b = centred(streams_of[10], (EXPERTS, HID), 0.5, 3.0, ((0, 2),), jnp.float32)
    gate_w = centred(streams_of[11], (EIN, TASKS, EXPERTS), EIN ** -0.5, 0.1875)
    return {"ids": ids, "bag_len": bag_len, "slot_of_feature": slot_of_feature, "tables": tables, "cross_w": cross_w, "cross_b": cross_b, "comp_w": comp_w, "comp_b": comp_b, "other_towers": other_towers, "expert_w": expert_w, "expert_b": expert_b, "gate_w": gate_w}


def pool_feature(lookup, indices, lengths):
    gathered = jnp.take(lookup, indices, axis=0)
    in_bag = jnp.arange(indices.shape[1])[None, :] < lengths[:, None]
    summed = jnp.sum(jnp.where(in_bag[:, :, None], gathered.astype(jnp.float32), 0.0), axis=1)
    return summed.astype(jnp.bfloat16)


def reference(ids, bag_len, slot_of_feature, tables, cross_w, cross_b, comp_w, comp_b, other_towers, expert_w, expert_b, gate_w):
    flat_tables = tables.reshape(TOWERS * NF, VOCAB, ED)
    flat_ids = ids.reshape(TOWERS * NF, SAMPLES, BAG)
    flat_len = bag_len.reshape(TOWERS * NF, SAMPLES)
    pooled = lax.map(lambda packed: pool_feature(packed[0], packed[1], packed[2]), (flat_tables, flat_ids, flat_len))
    pooled = pooled.reshape(TOWERS, NF, SAMPLES, ED)
    outputs = []
    for tower in range(TOWERS):
        onehot = (slot_of_feature[tower][:, None] == jnp.arange(NF)[None, :]).astype(jnp.float32)
        first_layer = jnp.einsum('fsd,fg->sgd', pooled[tower].astype(jnp.float32), onehot).astype(jnp.bfloat16).reshape(SAMPLES, WIDTH)
        crossed = jnp.dot(first_layer, cross_w[tower], preferred_element_type=jnp.float32) + cross_b[tower]
        base = first_layer.astype(jnp.float32)
        next_layer = (base * crossed + base).astype(jnp.bfloat16)
        squeezed = jnp.dot(next_layer, comp_w[tower], preferred_element_type=jnp.float32) + comp_b[tower]
        outputs.append(squeezed.astype(jnp.bfloat16))
    expert_in = jnp.concatenate([other_towers] + outputs, axis=1)
    logits = jnp.einsum('ri,ike->rke', expert_in.astype(jnp.float32), gate_w.astype(jnp.float32))
    weights = jnp.exp(logits)
    gate_probs = weights / jnp.sum(weights, axis=2, keepdims=True)

    def add_expert(running, packed):
        matrix, bias, member = packed
        hidden = jnp.maximum(jnp.dot(expert_in, matrix, preferred_element_type=jnp.float32) + bias, 0.0).astype(jnp.bfloat16)
        chosen = jnp.sum(gate_probs * (jnp.arange(EXPERTS) == member).astype(jnp.float32)[None, None, :], axis=2)
        return running + chosen[:, :, None] * hidden.astype(jnp.float32)[:, None, :], None

    start = jnp.zeros((SAMPLES, TASKS, HID), jnp.float32)
    running, unused = lax.scan(add_expert, start, (expert_w, expert_b, jnp.arange(EXPERTS).astype(jnp.int32)))
    return running.astype(jnp.bfloat16)
```

```python
import functools

import jax
import jax.numpy as jnp
from jax import lax
from jax.experimental import pallas as pl
from jax.experimental.pallas import tpu as pltpu
from jax.sharding import PartitionSpec as P

LOW = 256


def gather_kernel(low, tile, ids_ref, len_ref, tab_ref, out_ref, rows_ref):
    feature = pl.program_id(0)
    embed, vocab = tab_ref.shape[1], tab_ref.shape[2]
    bag, samples = ids_ref.shape[1], ids_ref.shape[2]
    row_count = out_ref.shape[3]
    high = vocab // low
    for part in range(0, high, 2):
        pair = [tab_ref[0, :, pl.ds((part + n) * low, low)].astype(jnp.float32) for n in range(2)]
        rows_ref[pl.ds(part * embed, 2 * embed), :] = jnp.concatenate(pair, axis=0).astype(jnp.bfloat16)
    level = lax.broadcasted_iota(jnp.int32, (low, tile), 0)

    def one_tile(step, carry):
        start = pl.multiple_of(step * tile, tile)
        length = len_ref[pl.ds(feature, 1), pl.ds(start, tile)]
        total = jnp.zeros((embed, tile), jnp.float32)
        for slot in range(bag):
            index = ids_ref[feature, pl.ds(slot, 1), pl.ds(start, tile)]
            upper = jnp.where(slot < length, index // low, -1)
            chosen = (level == index % low).astype(jnp.float32).astype(jnp.bfloat16)
            found = jnp.dot(rows_ref[...], chosen, preferred_element_type=jnp.float32)
            picked = jnp.zeros((embed, tile), jnp.float32)
            for part in range(high):
                picked = jnp.where(upper == part, found[part * embed : (part + 1) * embed], picked)
            total = total + picked
        for block in range(tile // row_count):
            piece = total[:, block * row_count : (block + 1) * row_count]
            out_ref[step * (tile // row_count) + block, feature] = piece.astype(jnp.bfloat16)
        return carry

    lax.fori_loop(0, samples // tile, one_tile, 0)


def pool_features(table, ids, lengths, inner_size):
    features, embed, vocab = table.shape
    bag, samples = ids.shape[1], ids.shape[2]
    row_count = samples // inner_size
    tile = row_count * max(1, 512 // row_count)
    whole = lambda shape: pl.BlockSpec(shape, lambda f: (0,) * len(shape))
    out_shape = (inner_size, features, embed, row_count)
    return pl.pallas_call(
        functools.partial(gather_kernel, LOW, tile),
        out_shape=jax.ShapeDtypeStruct(out_shape, jnp.bfloat16),
        grid=(features,),
        in_specs=[
            whole(ids.shape),
            whole(lengths.shape),
            pl.BlockSpec((1, embed, vocab), lambda f: (f, 0, 0)),
        ],
        out_specs=whole(out_shape),
        scratch_shapes=[pltpu.VMEM((vocab // LOW * embed, LOW), jnp.bfloat16)],
        compiler_params=pltpu.CompilerParams(vmem_limit_bytes=40 * 2**20),
        name="pool_features",
    )(ids, lengths, table)


def cross_kernel(blocks, slot_ref, rec_ref, w_hbm, bias_ref, comp_ref, comp_bias_ref, out_ref, first_t, first, w_ref, sems):
    slots, embed, rows = rec_ref.shape
    width = w_ref.shape[1]
    step = width // blocks
    copies = []
    for n in range(blocks):
        span = pl.ds(n * step, step)
        copies.append(pltpu.make_async_copy(w_hbm.at[:, span], w_ref.at[:, span], sems.at[n]))
        copies[-1].start()
    for f in range(slots):
        first_t[slot_ref[f]] = rec_ref[f].astype(jnp.float32)
    first[...] = first_t[...].reshape(width, rows).T.astype(jnp.bfloat16)
    total = jnp.zeros((rows, comp_ref.shape[0]), jnp.float32) + comp_bias_ref[...]
    for n in range(blocks):
        span = pl.ds(n * step, step)
        copies[n].wait()
        crossed = jnp.dot(first[...], w_ref[:, span], preferred_element_type=jnp.float32) + bias_ref[:, span]
        base = first[:, span].astype(jnp.float32)
        second = (base * crossed + base).astype(jnp.bfloat16)
        total = total + lax.dot_general(
            second, comp_ref[:, span], (((1,), (1,)), ((), ())), preferred_element_type=jnp.float32
        )
    out_ref[...] = total.astype(jnp.bfloat16)


def cross_and_compress(received, slots, cross_w, cross_b, comp_w, comp_b):
    slot_total, embed, rows = received.shape
    width = cross_w.shape[0]
    blocks = width // 256
    vmem = pl.BlockSpec(memory_space=pltpu.VMEM)
    return pl.pallas_call(
        functools.partial(cross_kernel, blocks),
        out_shape=jax.ShapeDtypeStruct((rows, comp_w.shape[1]), jnp.bfloat16),
        in_specs=[pl.BlockSpec(memory_space=pltpu.SMEM), vmem, pl.BlockSpec(memory_space=pl.ANY), vmem, vmem, vmem],
        out_specs=vmem,
        scratch_shapes=[
            pltpu.VMEM((slot_total, embed, rows), jnp.float32),
            pltpu.VMEM((rows, width), jnp.bfloat16),
            pltpu.VMEM((width, width), jnp.bfloat16),
            pltpu.SemaphoreType.DMA((blocks,)),
        ],
        compiler_params=pltpu.CompilerParams(vmem_limit_bytes=16 * 2**20),
        name="cross_and_compress",
    )(slots, received, cross_w, cross_b, comp_w.T, comp_b)


def mix_kernel(tower_ref, early_ref, late_w_ref, bias_ref, gate_early_ref, gate_late_ref, own_ref, other_ref, out_ref):
    experts, rows, columns = early_ref.shape
    tasks = gate_early_ref.shape[1] // experts
    mine, other = own_ref[...], other_ref[...]
    lead = tower_ref[0] == 0
    squeezed = jnp.concatenate([jnp.where(lead, mine, other), jnp.where(lead, other, mine)], axis=1)
    logits = gate_early_ref[...] + jnp.dot(squeezed, gate_late_ref[...], preferred_element_type=jnp.float32)
    weights = jnp.exp(logits)
    norm = sum(weights[:, e * tasks : (e + 1) * tasks] for e in range(experts))
    probs = [weights[:, e * tasks : (e + 1) * tasks] / norm for e in range(experts)]
    totals = [jnp.zeros((rows, columns), jnp.float32) for _ in range(tasks)]
    for e in range(experts):
        hidden = early_ref[e] + jnp.dot(squeezed, late_w_ref[e], preferred_element_type=jnp.float32)
        hidden = jnp.maximum(hidden + bias_ref[pl.ds(e, 1), :], 0.0).astype(jnp.bfloat16).astype(jnp.float32)
        for k in range(tasks):
            totals[k] = totals[k] + probs[e][:, k : k + 1] * hidden
    for k in range(tasks):
        out_ref[:, pl.ds(k * columns, columns)] = totals[k].astype(jnp.bfloat16)


def mix_experts(tower, early, late_w, bias, gate_early, gate_late, own, other):
    experts, rows, columns = early.shape
    tasks = gate_early.shape[1] // experts
    vmem = pl.BlockSpec(memory_space=pltpu.VMEM)
    out = pl.pallas_call(
        mix_kernel,
        out_shape=jax.ShapeDtypeStruct((rows, tasks * columns), jnp.bfloat16),
        in_specs=[pl.BlockSpec(memory_space=pltpu.SMEM)] + [vmem] * 7,
        out_specs=vmem,
        compiler_params=pltpu.CompilerParams(vmem_limit_bytes=16 * 2**20),
        name="mix_experts",
    )(tower, early, late_w, bias, gate_early, gate_late, own, other)
    return out.reshape(rows, tasks, columns)


def on_device(
    ids,
    bag_len,
    slot_of_feature,
    tables,
    cross_w,
    cross_b,
    comp_w,
    comp_b,
    other_towers,
    expert_w,
    expert_b,
    gate_w,
):
    inner_size = lax.axis_size("inner")
    tower_size = lax.axis_size("tower")
    tower = lax.axis_index("tower")
    swap = [(n, (n + 1) % tower_size) for n in range(tower_size)]

    far_w = lax.ppermute(expert_w, "tower", swap)
    far_b = lax.ppermute(expert_b, "tower", swap)

    pooled = pool_features(
        jnp.transpose(tables[0], (0, 2, 1)), jnp.transpose(ids[0], (0, 2, 1)), bag_len[0], inner_size
    )
    received = lax.all_to_all(pooled, "inner", split_axis=0, concat_axis=0, tiled=True)
    received = received.reshape((-1,) + received.shape[2:])

    exp_local, expert_in, hidden_width = expert_w.shape
    columns = hidden_width // tower_size
    known = other_towers.shape[1]
    half = lambda x: lax.dynamic_slice_in_dim(x, tower * columns, columns, axis=x.ndim - 1)
    both_w = jnp.concatenate([half(expert_w), half(far_w)], axis=0)
    both_b = jnp.concatenate([half(expert_b), half(far_b)], axis=0)
    early = jnp.einsum("ri,eih->erh", other_towers, both_w[:, :known], preferred_element_type=jnp.float32)
    task_count, expert_count = gate_w.shape[1:]
    gates = jnp.roll(jnp.transpose(gate_w, (2, 1, 0)), -tower * exp_local, axis=0)
    gates = gates.reshape(expert_count * task_count, expert_in)
    gate_early = lax.dot_general(
        other_towers, gates[:, :known], (((1,), (1,)), ((), ())), preferred_element_type=jnp.float32
    )
    gate_late = gates[:, known:].T

    squeezed = cross_and_compress(received, slot_of_feature[0], cross_w[0], cross_b, comp_w[0], comp_b)
    opposite = lax.ppermute(squeezed, "tower", swap)
    return mix_experts(
        tower.reshape(1), early, both_w[:, known:], both_b, gate_early, gate_late, squeezed, opposite
    )


def solution(mesh):
    return jax.shard_map(
        on_device,
        mesh=mesh,
        in_specs=(
            P("tower", "inner", "groups", None),
            P("tower", "inner", "groups"),
            P("tower", None),
            P("tower", "inner", None, None),
            P("tower", None, None),
            P("tower", None),
            P("tower", None, None),
            P("tower", None),
            P(("groups", "inner"), None),
            P("tower", None, None),
            P("tower", None),
            P(),
        ),
        out_specs=P(("groups", "inner"), None, "tower"),
        check_vma=False,
    )
```

```python
import functools

import jax
import jax.numpy as jnp
from jax import lax
from jax.experimental import pallas as pl
from jax.experimental.pallas import tpu as pltpu
from jax.sharding import PartitionSpec as P

LOW = 256
CHUNKS = 4


def pool_kernel(by_row, tile, row_count, groups, *refs):
    ids_hbm, len_hbm, tab_hbm, out_ref, ids_ref, len_ref, tab, table_low, sem = refs[:9]
    features, embed, vocab = tab.shape
    bag, samples = ids_ref.shape[1], ids_ref.shape[2]
    high = vocab // LOW
    copies = [pltpu.make_async_copy(ids_hbm, ids_ref, sem.at[0]), pltpu.make_async_copy(len_hbm, len_ref, sem.at[1])]
    for copy in copies:
        copy.start()
    parts = []
    if by_row:
        row_ref, pooled, shown, sem_ids = refs[9:13]
        addresses = refs[13:]
        width = vocab // CHUNKS
        for c in range(CHUNKS):
            where = (pl.ds(0, by_row), slice(None), pl.ds(c * width, width))
            parts.append(pltpu.make_async_copy(tab_hbm.at[where], tab.at[where], sem.at[3 + c]))
            parts[-1].start()
    others = pl.ds(by_row, features - by_row)
    rest_copy = pltpu.make_async_copy(tab_hbm.at[others], tab.at[others], sem.at[2])
    rest_copy.start()
    for copy in copies:
        copy.wait()
    if by_row:
        for f in range(by_row):
            for j in range(bag):
                shown[f * bag + j] = jnp.where(j < len_ref[pl.ds(f, 1), :], ids_ref[f, pl.ds(j, 1), :], vocab)
        moves = [pltpu.make_async_copy(shown.at[n, 0], addresses[n], sem_ids.at[n]) for n in range(by_row * bag)]
        for move in moves:
            move.start()
        row_ref[pl.ds(vocab, 8), :] = jnp.zeros((8, 128), jnp.float32)
        square = [lax.broadcasted_iota(jnp.int32, (LOW, LOW), axis) for axis in range(2)]
        unit = (square[0] == square[1]).astype(jnp.float32).astype(jnp.bfloat16)
        blank = jnp.zeros((128 - by_row * embed, LOW), jnp.float32)

        def build(block, carry, first):
            start = pl.multiple_of(first + block * 2 * LOW, 2 * LOW)
            both = []
            for n in range(2):
                both += [tab[f, :, pl.ds(start + n * LOW, LOW)].astype(jnp.float32) for f in range(by_row)] + [blank]
            columns = jnp.concatenate(both, axis=0).astype(jnp.bfloat16)
            turned = lax.dot_general(unit, columns, (((1,), (1,)), ((), ())), preferred_element_type=jnp.float32)
            row_ref[pl.ds(start, LOW), :] = turned[:, :128]
            row_ref[pl.ds(start + LOW, LOW), :] = turned[:, 128:]
            return carry

        for c in range(CHUNKS):
            parts[c].wait()
            lax.fori_loop(0, width // (2 * LOW), functools.partial(build, first=c * width), 0, unroll=4)
        for move in moves:
            move.wait()
    rest_copy.wait()
    lane = lax.broadcasted_iota(jnp.int32, (1, 128), 1)

    def lookups(group):
        row = pl.multiple_of(group * 8, 8)
        for u in range(8):
            line = None
            for f in range(by_row):
                found = [row_ref[pl.ds(addresses[f * bag + j][row + u], 1), :] for j in range(bag)]
                total = found[0]
                for item in found[1:]:
                    total = total + item
                line = total if line is None else jnp.where(lane < embed * f, line, total)
                yield
            pooled[pl.ds(row + u, 1), :] = line

    level = lax.broadcasted_iota(jnp.int32, (LOW, tile), 0)
    tiles = samples // tile
    last = samples // 8 - 1

    def step(i, carry):
        feature, t = by_row + i // tiles, i % tiles
        start = pl.multiple_of(t * tile, tile)

        def arrange():
            for part in range(0, high, 2):
                pair = [tab[feature, :, pl.ds((part + n) * LOW, LOW)].astype(jnp.float32) for n in range(2)]
                table_low[pl.ds(part * embed, 2 * embed), :] = jnp.concatenate(pair, axis=0).astype(jnp.bfloat16)

        pl.when(t == 0)(arrange)
        work = (item for g in range(groups) for item in lookups(jnp.minimum(i * groups + g, last)))
        wanted = groups * 8 * by_row
        given, selects = 0, 0
        length = len_ref[pl.ds(feature, 1), pl.ds(start, tile)]
        total = jnp.zeros((embed, tile), jnp.float32)
        for slot in range(bag):
            index = ids_ref[feature, pl.ds(slot, 1), pl.ds(start, tile)]
            upper = jnp.where(slot < length, index // LOW, -1)
            chosen = (level == index % LOW).astype(jnp.float32).astype(jnp.bfloat16)
            found = jnp.dot(table_low[...], chosen, preferred_element_type=jnp.float32)
            picked = jnp.zeros((embed, tile), jnp.float32)
            for part in range(high):
                picked = jnp.where(upper == part, found[part * embed : (part + 1) * embed], picked)
                selects += 1
                while given * bag * high < selects * wanted:
                    next(work, None)
                    given += 1
            total = total + picked
        for _ in work:
            pass
        for block in range(tile // row_count):
            piece = total[:, block * row_count : (block + 1) * row_count]
            out_ref[t * (tile // row_count) + block, feature] = piece.astype(jnp.bfloat16)
        return carry

    steps = (features - by_row) * tiles
    lax.fori_loop(0, steps, step, 0)
    if by_row:

        def rest(group, carry):
            for _ in lookups(group):
                pass
            return carry

        lax.fori_loop(min(steps * groups, last + 1), last + 1, rest, 0)
        for block in range(samples // row_count):
            turned = pooled[pl.ds(block * row_count, row_count), :].T
            for f in range(by_row):
                out_ref[block, f] = turned[f * embed : (f + 1) * embed].astype(jnp.bfloat16)


def pool_features(table, ids, lengths, inner_size):
    features, embed, vocab = table.shape
    bag, samples = ids.shape[1], ids.shape[2]
    row_count = samples // inner_size
    tile = row_count * max(1, min(samples, 1024) // row_count)
    by_row = min(128 // embed, features * 5 // 8)
    steps = (features - by_row) * (samples // tile)
    groups = samples // 8 // steps * 15 // 16 if by_row else 0
    hbm = pl.BlockSpec(memory_space=pltpu.HBM)
    scratch = [
        pltpu.VMEM(ids.shape, jnp.int32),
        pltpu.VMEM(lengths.shape, jnp.int32),
        pltpu.VMEM(table.shape, jnp.bfloat16),
        pltpu.VMEM((vocab // LOW * embed, LOW), jnp.bfloat16),
        pltpu.SemaphoreType.DMA((3 + CHUNKS,)),
    ]
    if by_row:
        scratch += [
            pltpu.VMEM((vocab + 8, 128), jnp.float32),
            pltpu.VMEM((samples, 128), jnp.float32),
            pltpu.VMEM((by_row * bag, 1, samples), jnp.int32),
            pltpu.SemaphoreType.DMA((by_row * bag,)),
        ] + [pltpu.SMEM((samples,), jnp.int32)] * (by_row * bag)
    return pl.pallas_call(
        functools.partial(pool_kernel, by_row, tile, row_count, groups),
        out_shape=jax.ShapeDtypeStruct((inner_size, features, embed, row_count), jnp.bfloat16),
        in_specs=[hbm, hbm, hbm],
        out_specs=pl.BlockSpec(memory_space=pltpu.VMEM),
        scratch_shapes=scratch,
        compiler_params=pltpu.CompilerParams(vmem_limit_bytes=48 * 2**20),
        name="pool_features",
    )(ids, lengths, table)


def early_kernel(known, tower_ref, other_ref, own_hbm, far_hbm, own_bias_ref, far_bias_ref, gate_ref, cross_hbm, *refs):
    early_ref, gate_early_ref, late_ref, gate_late_ref, cross_ref, weights, sem = refs
    tower = tower_ref[0]
    half, experts_in, columns = own_hbm.shape[0], weights.shape[1], weights.shape[2]
    span = pl.ds(pl.multiple_of(tower * columns, columns), columns)
    copies = []
    for n, (source, place) in enumerate([(own_hbm, tower), (far_hbm, 1 - tower)]):
        for e in range(half):
            copies.append(
                pltpu.make_async_copy(source.at[e, :, span], weights.at[place * half + e], sem.at[n * half + e])
            )
            copies[-1].start()
    cross_copy = pltpu.make_async_copy(cross_hbm, cross_ref, sem.at[2 * half])
    cross_copy.start()
    tasks, experts, depth = gate_ref.shape
    gates = gate_ref[...].astype(jnp.float32).reshape(tasks * experts, depth).astype(jnp.bfloat16)
    gate_early_ref[...] = lax.dot_general(
        other_ref[...], gates[:, :known], (((1,), (1,)), ((), ())), preferred_element_type=jnp.float32
    )
    gate_late_ref[...] = gates[:, known:]
    for n, (bias, place) in enumerate([(own_bias_ref, tower), (far_bias_ref, 1 - tower)]):
        for e in range(half):
            copies[n * half + e].wait()
            at = place * half + e
            found = jnp.dot(other_ref[...], weights[at, pl.ds(0, known), :], preferred_element_type=jnp.float32)
            early_ref[at] = found + bias[pl.ds(e, 1), span]
            late_ref[at] = weights[at, pl.ds(known, experts_in - known), :]
    cross_copy.wait()


def early_part(tower, other, own_w, far_w, own_b, far_b, gates, cross_w):
    half, depth, hidden = own_w.shape
    rows, known = other.shape
    columns = hidden // 2
    vmem, hbm = pl.BlockSpec(memory_space=pltpu.VMEM), pl.BlockSpec(memory_space=pltpu.HBM)
    count = gates.shape[0] * gates.shape[1]
    return pl.pallas_call(
        functools.partial(early_kernel, known),
        out_shape=(
            jax.ShapeDtypeStruct((2 * half, rows, columns), jnp.float32),
            jax.ShapeDtypeStruct((rows, count), jnp.float32),
            jax.ShapeDtypeStruct((2 * half, depth - known, columns), jnp.bfloat16),
            jax.ShapeDtypeStruct((count, depth - known), jnp.bfloat16),
            jax.ShapeDtypeStruct(cross_w.shape, jnp.bfloat16),
        ),
        in_specs=[pl.BlockSpec(memory_space=pltpu.SMEM), vmem, hbm, hbm, vmem, vmem, vmem, hbm],
        out_specs=(vmem,) * 5,
        scratch_shapes=[pltpu.VMEM((2 * half, depth, columns), jnp.bfloat16), pltpu.SemaphoreType.DMA((2 * half + 1,))],
        compiler_params=pltpu.CompilerParams(vmem_limit_bytes=24 * 2**20),
        cost_estimate=pl.CostEstimate(
            flops=4 * half * rows * known * columns,
            bytes_accessed=2 * (2 * half * depth * columns + cross_w.size),
            transcendentals=0,
        ),
        name="early_part",
    )(tower, other, own_w, far_w, own_b, far_b, gates, cross_w)


def cross_kernel(blocks, slot_ref, rec_ref, w_ref, bias_ref, comp_ref, comp_bias_ref, out_ref, first_t, first):
    slots, embed, rows = rec_ref.shape
    width = w_ref.shape[1]
    step = width // blocks
    for f in range(slots):
        first_t[slot_ref[f]] = rec_ref[f].astype(jnp.float32)
    first[...] = first_t[...].reshape(width, rows).T.astype(jnp.bfloat16)
    total = jnp.zeros((rows, comp_ref.shape[0]), jnp.float32) + comp_bias_ref[...]
    for n in range(blocks):
        span = pl.ds(n * step, step)
        crossed = jnp.dot(first[...], w_ref[:, span], preferred_element_type=jnp.float32) + bias_ref[:, span]
        base = first[:, span].astype(jnp.float32)
        second = (base * crossed + base).astype(jnp.bfloat16)
        total = total + lax.dot_general(
            second, comp_ref[:, span], (((1,), (1,)), ((), ())), preferred_element_type=jnp.float32
        )
    out_ref[...] = total.astype(jnp.bfloat16)


def cross_and_compress(received, slots, cross_w, cross_b, comp_w, comp_b):
    slot_total, embed, rows = received.shape
    width = cross_w.shape[0]
    vmem = pl.BlockSpec(memory_space=pltpu.VMEM)
    return pl.pallas_call(
        functools.partial(cross_kernel, width // 256),
        out_shape=jax.ShapeDtypeStruct((rows, comp_w.shape[1]), jnp.bfloat16),
        in_specs=[pl.BlockSpec(memory_space=pltpu.SMEM), vmem, vmem, vmem, vmem, vmem],
        out_specs=vmem,
        scratch_shapes=[
            pltpu.VMEM((slot_total, embed, rows), jnp.float32),
            pltpu.VMEM((rows, width), jnp.bfloat16),
        ],
        compiler_params=pltpu.CompilerParams(vmem_limit_bytes=16 * 2**20),
        name="cross_and_compress",
    )(slots, received, cross_w, cross_b, comp_w.T, comp_b)


def mix_kernel(tower_ref, early_ref, late_ref, gate_early_ref, gate_late_ref, own_ref, far_ref, out_ref):
    experts, rows, columns = early_ref.shape
    tasks = gate_early_ref.shape[1] // experts
    own, far = own_ref[...], far_ref[...]
    lead = tower_ref[0] == 0
    squeezed = jnp.concatenate([jnp.where(lead, own, far), jnp.where(lead, far, own)], axis=1)
    logits = gate_early_ref[...] + lax.dot_general(
        squeezed, gate_late_ref[...], (((1,), (1,)), ((), ())), preferred_element_type=jnp.float32
    )
    weights = jnp.exp(logits)
    probs = []
    for k in range(tasks):
        mine = weights[:, k * experts : (k + 1) * experts]
        probs.append(mine / jnp.sum(mine, axis=1, keepdims=True))
    totals = [jnp.zeros((rows, columns), jnp.float32) for _ in range(tasks)]
    for e in range(experts):
        hidden = early_ref[e] + jnp.dot(squeezed, late_ref[e], preferred_element_type=jnp.float32)
        hidden = jnp.maximum(hidden, 0.0).astype(jnp.bfloat16).astype(jnp.float32)
        for k in range(tasks):
            totals[k] = totals[k] + probs[k][:, e : e + 1] * hidden
    out_ref[...] = jnp.stack(totals, axis=1).astype(jnp.bfloat16)


def mix_experts(tower, early, late, gate_early, gate_late, own, far):
    experts, rows, columns = early.shape
    tasks = gate_early.shape[1] // experts
    vmem = pl.BlockSpec(memory_space=pltpu.VMEM)
    return pl.pallas_call(
        mix_kernel,
        out_shape=jax.ShapeDtypeStruct((rows, tasks, columns), jnp.bfloat16),
        in_specs=[pl.BlockSpec(memory_space=pltpu.SMEM)] + [vmem] * 6,
        out_specs=vmem,
        compiler_params=pltpu.CompilerParams(vmem_limit_bytes=16 * 2**20),
        name="mix_experts",
    )(tower, early, late, gate_early, gate_late, own, far)


def on_device(
    ids,
    bag_len,
    slot_of_feature,
    tables,
    cross_w,
    cross_b,
    comp_w,
    comp_b,
    other_towers,
    expert_w,
    expert_b,
    gate_w,
):
    inner_size = lax.axis_size("inner")
    tower_size = lax.axis_size("tower")
    tower = lax.axis_index("tower")
    swap = [(n, (n + 1) % tower_size) for n in range(tower_size)]

    far_w = lax.ppermute(expert_w, "tower", swap)
    far_b = lax.ppermute(expert_b, "tower", swap)

    pooled = pool_features(
        jnp.transpose(tables[0], (0, 2, 1)), jnp.transpose(ids[0], (0, 2, 1)), bag_len[0], inner_size
    )
    received = lax.all_to_all(pooled, "inner", split_axis=0, concat_axis=0, tiled=True)
    received = received.reshape((-1,) + received.shape[2:])

    place = tower.reshape(1)
    gates = jnp.transpose(gate_w, (1, 2, 0))
    early = early_part(place, other_towers, expert_w, far_w, expert_b, far_b, gates, cross_w[0])
    received, early = lax.optimization_barrier((received, early))
    hidden_early, gate_early, late_w, gate_late, near_w = early

    squeezed = cross_and_compress(received, slot_of_feature[0], near_w, cross_b, comp_w[0], comp_b)
    opposite = lax.ppermute(squeezed, "tower", swap)
    return mix_experts(place, hidden_early, late_w, gate_early, gate_late, squeezed, opposite)


def solution(mesh):
    return jax.shard_map(
        on_device,
        mesh=mesh,
        in_specs=(
            P("tower", "inner", "groups", None),
            P("tower", "inner", "groups"),
            P("tower", None),
            P("tower", "inner", None, None),
            P("tower", None, None),
            P("tower", None),
            P("tower", None, None),
            P("tower", None),
            P(("groups", "inner"), None),
            P("tower", None, None),
            P("tower", None),
            P(),
        ),
        out_specs=P(("groups", "inner"), None, "tower"),
        check_vma=False,
    )
```

```python
import functools
import math

import jax
import jax.numpy as jnp
from jax import lax
from jax.experimental import pallas as pl
from jax.experimental.pallas import tpu as pltpu
from jax.sharding import PartitionSpec as P

LOW = 256
CHUNKS = 4
PAIR = 1
OWN = 5


def arrange_low(table_low, tab, feature):
    embed, vocab = tab.shape[1], tab.shape[2]
    for part in range(0, vocab // LOW, 2):
        pair = [tab[feature, :, pl.ds((part + n) * LOW, LOW)].astype(jnp.float32) for n in range(2)]
        table_low[pl.ds(part * embed, 2 * embed), :] = jnp.concatenate(pair, axis=0).astype(jnp.bfloat16)


def pool_matched(table_low, high, index, between=None):
    rows, bag = index[0].shape[1], len(index)
    embed = table_low.shape[0] // high
    total = None
    for first in range(0, bag, PAIR):
        ids = jnp.concatenate(index[first : first + PAIR], axis=1)
        width = ids.shape[1]
        upper, lower = ids // LOW, ids % LOW
        level = lax.broadcasted_iota(jnp.int32, (LOW, width), 0)
        chosen = (level == lower).astype(jnp.float32).astype(jnp.bfloat16)
        found = jnp.dot(table_low[...], chosen, preferred_element_type=jnp.float32)
        picked = jnp.zeros((embed, width), jnp.float32)
        for part in range(high):
            picked = jnp.where(upper == part, found[part * embed : (part + 1) * embed], picked)
            if between is not None:
                between()
        for j in range(width // rows):
            piece = picked[:, j * rows : (j + 1) * rows]
            total = piece if total is None else total + piece
    return total


def pool_kernel(by_row, tile, groups, row_count, *refs):
    me_ref, ids_hbm, len_hbm, tab_hbm, out_ref, ids_ref, len_ref, shown, tab, table_low, sem = refs[:11]
    features, embed, vocab = tab.shape
    bag, samples = ids_ref.shape[1], ids_ref.shape[2]
    dests = samples // row_count
    high = vocab // LOW
    me = me_ref[0]
    copies = [pltpu.make_async_copy(ids_hbm, ids_ref, sem.at[0]), pltpu.make_async_copy(len_hbm, len_ref, sem.at[1])]
    for copy in copies:
        copy.start()
    parts = []
    if by_row:
        row_ref, pooled, sem_ids = refs[11:14]
        addresses = refs[14:]
        width = vocab // CHUNKS
        for c in range(CHUNKS):
            where = (pl.ds(0, by_row), slice(None), pl.ds(c * width, width))
            parts.append(pltpu.make_async_copy(tab_hbm.at[where], tab.at[where], sem.at[3 + c]))
            parts[-1].start()
    others = pl.ds(by_row, features - by_row)
    rest_copy = pltpu.make_async_copy(tab_hbm.at[others], tab.at[others], sem.at[2])
    rest_copy.start()
    for copy in copies:
        copy.wait()
    for f in range(features):
        for j in range(bag):
            shown[f * bag + j] = jnp.where(j < len_ref[pl.ds(f, 1), :], ids_ref[f, pl.ds(j, 1), :], vocab)
    if by_row:
        moves = [pltpu.make_async_copy(shown.at[n, 0], addresses[n], sem_ids.at[n]) for n in range(by_row * bag)]
        for move in moves:
            move.start()
        row_ref[pl.ds(vocab, 8), :] = jnp.zeros((8, 128), jnp.float32)
        square = [lax.broadcasted_iota(jnp.int32, (LOW, LOW), axis) for axis in range(2)]
        unit = (square[0] == square[1]).astype(jnp.float32).astype(jnp.bfloat16)
        blank = jnp.zeros((128 - by_row * embed, LOW), jnp.float32)

        def build(block, carry, first):
            start = pl.multiple_of(first + block * 2 * LOW, 2 * LOW)
            both = []
            for n in range(2):
                both += [tab[f, :, pl.ds(start + n * LOW, LOW)].astype(jnp.float32) for f in range(by_row)] + [blank]
            columns = jnp.concatenate(both, axis=0).astype(jnp.bfloat16)
            turned = lax.dot_general(unit, columns, (((1,), (1,)), ((), ())), preferred_element_type=jnp.float32)
            row_ref[pl.ds(start, LOW), :] = turned[:, :128]
            row_ref[pl.ds(start + LOW, LOW), :] = turned[:, 128:]
            return carry

        for c in range(CHUNKS):
            parts[c].wait()
            lax.fori_loop(0, width // (2 * LOW), functools.partial(build, first=c * width), 0, unroll=4)
        for move in moves:
            move.wait()
    rest_copy.wait()
    lane = lax.broadcasted_iota(jnp.int32, (1, 128), 1)

    def other(block):
        dest = me + 1 + block
        return jnp.where(dest >= dests, dest - dests, dest)

    def lookups(group):
        eighths = row_count // 8
        row = pl.multiple_of(other(group // eighths) * row_count + group % eighths * 8, 8)
        for u in range(8):
            line = None
            for f in range(by_row):
                found = [row_ref[pl.ds(addresses[f * bag + j][row + u], 1), :] for j in range(bag)]
                total = found[0]
                for item in found[1:]:
                    total = total + item
                line = total if line is None else jnp.where(lane < embed * f, line, total)
                yield
            pooled[pl.ds(row + u, 1), :] = line

    last = (dests - 1) * row_count // 8 - 1
    tiles = samples // tile

    def step(i, carry):
        feature, t = by_row + i // tiles, i % tiles
        pl.when(t == 0)(functools.partial(arrange_low, table_low, tab, feature))
        work = (item for g in range(groups) for item in lookups(jnp.minimum(i * groups + g, last)))
        wanted = groups * 8 * by_row
        count = [0, 0]

        def between():
            count[0] += 1
            while count[1] * (bag // PAIR) * high < count[0] * wanted:
                next(work, None)
                count[1] += 1

        span = pl.ds(pl.multiple_of(t * tile, tile), tile)
        index = [shown[feature * bag + j, :, span] for j in range(bag)]
        total = pool_matched(table_low, high, index, between)
        for block in range(tile // row_count):
            piece = total[:, block * row_count : (block + 1) * row_count]
            out_ref[t * (tile // row_count) + block, feature] = piece.astype(jnp.bfloat16)
        for _ in work:
            pass
        return carry

    steps = (features - by_row) * tiles
    lax.fori_loop(0, steps, step, 0)
    if by_row:

        def rest(group, carry):
            for _ in lookups(group):
                pass
            return carry

        lax.fori_loop(min(steps * groups, last + 1), last + 1, rest, 0)
    if by_row:
        out_ref[me, pl.ds(0, by_row)] = jnp.zeros((by_row, embed, row_count), jnp.bfloat16)

        def finish(block, carry):
            dest = other(block)
            turned = pooled[pl.ds(pl.multiple_of(dest * row_count, row_count), row_count), :].T
            for f in range(by_row):
                out_ref[dest, f] = turned[f * embed : (f + 1) * embed].astype(jnp.bfloat16)
            return carry

        lax.fori_loop(0, dests - 1, finish, 0, unroll=True)


def row_features(features, embed):
    return min(128 // embed, features * 5 // 8)


def pool_features(place, table, ids, lengths, inner_size):
    features, embed, vocab = table.shape
    bag, samples = ids.shape[1], ids.shape[2]
    row_count = samples // inner_size
    tile = row_count * max(1, min(samples, 1024) // row_count)
    by_row = row_features(features, embed)
    steps = (features - by_row) * (samples // tile)
    groups = -(-(samples - row_count) // 8 // steps) if by_row else 0
    hbm = pl.BlockSpec(memory_space=pltpu.HBM)
    scratch = [
        pltpu.VMEM(ids.shape, jnp.int32),
        pltpu.VMEM(lengths.shape, jnp.int32),
        pltpu.VMEM((features * bag, 1, samples), jnp.int32),
        pltpu.VMEM(table.shape, jnp.bfloat16),
        pltpu.VMEM((vocab // LOW * embed, LOW), jnp.bfloat16),
        pltpu.SemaphoreType.DMA((3 + CHUNKS,)),
    ]
    if by_row:
        scratch += [
            pltpu.VMEM((vocab + 8, 128), jnp.float32),
            pltpu.VMEM((samples, 128), jnp.float32),
            pltpu.SemaphoreType.DMA((by_row * bag,)),
        ] + [pltpu.SMEM((samples,), jnp.int32)] * (by_row * bag)
    return pl.pallas_call(
        functools.partial(pool_kernel, by_row, tile, groups, row_count),
        out_shape=pltpu.HBM((inner_size, features, embed, row_count), jnp.bfloat16),
        in_specs=[pl.BlockSpec(memory_space=pltpu.SMEM), hbm, hbm, hbm],
        out_specs=pl.BlockSpec(memory_space=pltpu.VMEM),
        scratch_shapes=scratch,
        compiler_params=pltpu.CompilerParams(vmem_limit_bytes=32 * 2**20),
        name="pool_features",
    )(place, *(pltpu.with_memory_space_constraint(x, pltpu.HBM) for x in (ids, lengths, table)))


def own_kernel(me_ref, ids_ref, len_ref, tab_ref, out_ref, *lows):
    together, vocab = len(lows), tab_ref.shape[2]
    for f, table_low in enumerate(lows):
        arrange_low(table_low, tab_ref, f)
        length = len_ref[pl.ds(pl.program_id(0) * together + f, 1), :]
        index = [jnp.where(j < length, ids_ref[f, pl.ds(j, 1), :], vocab) for j in range(ids_ref.shape[1])]
        out_ref[f] = pool_matched(table_low, vocab // LOW, index).astype(jnp.bfloat16)


def pool_own(place, table, ids, lengths, inner_size):
    all_features, embed, vocab = table.shape
    features = row_features(all_features, embed)
    bag, samples = ids.shape[1], ids.shape[2]
    rows = samples // inner_size
    together = math.gcd(features, OWN)
    return pl.pallas_call(
        own_kernel,
        out_shape=jax.ShapeDtypeStruct((features, embed, rows), jnp.bfloat16),
        grid_spec=pltpu.PrefetchScalarGridSpec(
            num_scalar_prefetch=1,
            grid=(features // together,),
            in_specs=[
                pl.BlockSpec((together, bag, rows), lambda f, me: (f, 0, me[0])),
                pl.BlockSpec((all_features, rows), lambda f, me: (0, me[0])),
                pl.BlockSpec((together, embed, vocab), lambda f, me: (f, 0, 0)),
            ],
            out_specs=pl.BlockSpec((together, embed, rows), lambda f, me: (f, 0, 0)),
            scratch_shapes=[pltpu.VMEM((vocab // LOW * embed, LOW), jnp.bfloat16)] * together,
        ),
        compiler_params=pltpu.CompilerParams(vmem_limit_bytes=16 * 2**20),
        cost_estimate=pl.CostEstimate(
            flops=2 * features * bag * rows * vocab * embed, bytes_accessed=2 * table.size, transcendentals=0
        ),
        name="pool_own",
    )(place, *(pltpu.with_memory_space_constraint(x, pltpu.HBM) for x in (ids, lengths, table)))


def early_kernel(known, tower_ref, other_ref, own_hbm, far_hbm, own_bias_ref, far_bias_ref, gate_ref, *refs):
    early_ref, gate_early_ref, late_ref, gate_late_ref, weights, sem = refs
    tower = tower_ref[0]
    half, experts_in, columns = own_hbm.shape[0], weights.shape[1], weights.shape[2]
    span = pl.ds(pl.multiple_of(tower * columns, columns), columns)
    copies = []
    for n, (source, place) in enumerate([(own_hbm, tower), (far_hbm, 1 - tower)]):
        for e in range(half):
            copies.append(
                pltpu.make_async_copy(source.at[e, :, span], weights.at[place * half + e], sem.at[n * half + e])
            )
            copies[-1].start()
    tasks, experts, depth = gate_ref.shape
    gates = gate_ref[...].astype(jnp.float32).reshape(tasks * experts, depth).astype(jnp.bfloat16)
    gate_early_ref[...] = lax.dot_general(
        other_ref[...], gates[:, :known], (((1,), (1,)), ((), ())), preferred_element_type=jnp.float32
    )
    gate_late_ref[...] = gates[:, known:]
    for n, (bias, place) in enumerate([(own_bias_ref, tower), (far_bias_ref, 1 - tower)]):
        for e in range(half):
            copies[n * half + e].wait()
            at = place * half + e
            found = jnp.dot(other_ref[...], weights[at, pl.ds(0, known), :], preferred_element_type=jnp.float32)
            early_ref[at] = found + bias[pl.ds(e, 1), span]
            late_ref[at] = weights[at, pl.ds(known, experts_in - known), :]


def early_part(tower, other, own_w, far_w, own_b, far_b, gates):
    half, depth, hidden = own_w.shape
    rows, known = other.shape
    columns = hidden // 2
    vmem, hbm = pl.BlockSpec(memory_space=pltpu.VMEM), pl.BlockSpec(memory_space=pltpu.HBM)
    count = gates.shape[0] * gates.shape[1]
    far = lambda x: pltpu.with_memory_space_constraint(x, pltpu.HBM)
    return pl.pallas_call(
        functools.partial(early_kernel, known),
        out_shape=(
            jax.ShapeDtypeStruct((2 * half, rows, columns), jnp.float32),
            jax.ShapeDtypeStruct((rows, count), jnp.float32),
            jax.ShapeDtypeStruct((2 * half, depth - known, columns), jnp.bfloat16),
            jax.ShapeDtypeStruct((count, depth - known), jnp.bfloat16),
        ),
        in_specs=[pl.BlockSpec(memory_space=pltpu.SMEM), vmem, hbm, hbm, vmem, vmem, vmem],
        out_specs=(vmem,) * 4,
        scratch_shapes=[pltpu.VMEM((2 * half, depth, columns), jnp.bfloat16), pltpu.SemaphoreType.DMA((2 * half,))],
        compiler_params=pltpu.CompilerParams(vmem_limit_bytes=16 * 2**20),
        cost_estimate=pl.CostEstimate(
            flops=4 * half * rows * known * columns,
            bytes_accessed=4 * half * depth * columns,
            transcendentals=0,
        ),
        name="early_part",
    )(tower, other, far(own_w), far_w, own_b, far_b, gates)


def cross_kernel(each, by_row, me_ref, slot_ref, rec_ref, own_ref, w_hbm, bias_ref, comp_ref, comp_bias_ref, *refs):
    out_ref, first_t, first, w_ref, sums, sem = refs
    slots, embed, rows = rec_ref.shape
    width, blocks = w_ref.shape[1], sem.shape[0]
    step = width // blocks
    spans = [pl.ds(n * step, step) for n in range(blocks)]
    copies = [pltpu.make_async_copy(w_hbm.at[span], w_ref.at[span], sem.at[n]) for n, span in enumerate(spans)]
    for copy in copies:
        copy.start()
    for f in range(slots):
        first_t[slot_ref[f]] = rec_ref[f].astype(jnp.float32)
    for f in range(by_row):
        first_t[slot_ref[me_ref[0] * each + f]] = own_ref[f].astype(jnp.float32)
    first[...] = first_t[...].reshape(width, rows).T.astype(jnp.bfloat16)
    crossed = bias_ref[...]
    for n, span in enumerate(spans):
        copies[n].wait()
        crossed = crossed + jnp.dot(first[:, span], w_ref[span, :], preferred_element_type=jnp.float32)
        if n + 1 < blocks:
            sums[...] = crossed
            crossed = sums[...]
    total = jnp.zeros((rows, comp_ref.shape[0]), jnp.float32) + comp_bias_ref[...]
    for n, span in enumerate(spans):
        base = first[:, span].astype(jnp.float32)
        second = (base * crossed[:, n * step : (n + 1) * step] + base).astype(jnp.bfloat16)
        total = total + lax.dot_general(
            second, comp_ref[:, span], (((1,), (1,)), ((), ())), preferred_element_type=jnp.float32
        )
    out_ref[...] = total.astype(jnp.bfloat16)


def cross_and_compress(place, slots, received, own, by_row, each, cross_w, cross_b, comp_w, comp_b):
    slot_total, embed, rows = received.shape
    width = cross_w.shape[0]
    vmem, smem = pl.BlockSpec(memory_space=pltpu.VMEM), pl.BlockSpec(memory_space=pltpu.SMEM)
    return pl.pallas_call(
        functools.partial(cross_kernel, each, by_row),
        out_shape=jax.ShapeDtypeStruct((rows, comp_w.shape[1]), jnp.bfloat16),
        in_specs=[smem, smem, vmem, vmem, pl.BlockSpec(memory_space=pltpu.HBM), vmem, vmem, vmem],
        out_specs=vmem,
        scratch_shapes=[
            pltpu.VMEM((slot_total, embed, rows), jnp.float32),
            pltpu.VMEM((rows, width), jnp.bfloat16),
            pltpu.VMEM(cross_w.shape, jnp.bfloat16),
            pltpu.VMEM((rows, width), jnp.float32),
            pltpu.SemaphoreType.DMA((width // 256,)),
        ],
        compiler_params=pltpu.CompilerParams(vmem_limit_bytes=16 * 2**20),
        name="cross_and_compress",
    )(place, slots, received, own, pltpu.with_memory_space_constraint(cross_w, pltpu.HBM), cross_b, comp_w.T, comp_b)


def mix_kernel(tower_ref, early_ref, late_ref, gate_early_ref, gate_late_ref, own_ref, far_ref, out_ref):
    experts, rows, columns = early_ref.shape
    tasks = gate_early_ref.shape[1] // experts
    own, far = own_ref[...], far_ref[...]
    lead = tower_ref[0] == 0
    squeezed = jnp.concatenate([jnp.where(lead, own, far), jnp.where(lead, far, own)], axis=1)
    logits = gate_early_ref[...] + lax.dot_general(
        squeezed, gate_late_ref[...], (((1,), (1,)), ((), ())), preferred_element_type=jnp.float32
    )
    weights = jnp.exp(logits)
    probs = []
    for k in range(tasks):
        mine = weights[:, k * experts : (k + 1) * experts]
        probs.append(mine / jnp.sum(mine, axis=1, keepdims=True))
    totals = [jnp.zeros((rows, columns), jnp.float32) for _ in range(tasks)]
    for e in range(experts):
        hidden = early_ref[e] + jnp.dot(squeezed, late_ref[e], preferred_element_type=jnp.float32)
        hidden = jnp.maximum(hidden, 0.0).astype(jnp.bfloat16).astype(jnp.float32)
        for k in range(tasks):
            totals[k] = totals[k] + probs[k][:, e : e + 1] * hidden
    out_ref[...] = jnp.stack(totals, axis=1).astype(jnp.bfloat16)


def mix_experts(tower, early, late, gate_early, gate_late, own, far):
    experts, rows, columns = early.shape
    tasks = gate_early.shape[1] // experts
    vmem = pl.BlockSpec(memory_space=pltpu.VMEM)
    return pl.pallas_call(
        mix_kernel,
        out_shape=jax.ShapeDtypeStruct((rows, tasks, columns), jnp.bfloat16),
        in_specs=[pl.BlockSpec(memory_space=pltpu.SMEM)] + [vmem] * 6,
        out_specs=vmem,
        compiler_params=pltpu.CompilerParams(vmem_limit_bytes=16 * 2**20),
        name="mix_experts",
    )(tower, early, late, gate_early, gate_late, own, far)


def on_device(
    ids,
    bag_len,
    slot_of_feature,
    tables,
    cross_w,
    cross_b,
    comp_w,
    comp_b,
    other_towers,
    expert_w,
    expert_b,
    gate_w,
):
    inner_size = lax.axis_size("inner")
    tower_size = lax.axis_size("tower")
    tower = lax.axis_index("tower")
    swap = [(n, (n + 1) % tower_size) for n in range(tower_size)]

    far_w = lax.ppermute(expert_w, "tower", swap)
    far_b = lax.ppermute(expert_b, "tower", swap)

    here = lax.axis_index("inner").reshape(1)
    tables_t, ids_t = jnp.transpose(tables[0], (0, 2, 1)), jnp.transpose(ids[0], (0, 2, 1))
    pooled = pool_features(here, tables_t, ids_t, bag_len[0], inner_size)
    dests, features, embed, rows = pooled.shape
    pooled = pooled.reshape(dests, features * embed, rows)
    received = lax.all_to_all(pooled, "inner", split_axis=0, concat_axis=0, tiled=True)
    received = received.reshape(dests * features, embed, rows)

    by_row = row_features(features, embed)
    own = pool_own(here, tables_t, ids_t, bag_len[0], inner_size) if by_row else received[:1]
    place = tower.reshape(1)
    gates = jnp.transpose(gate_w, (1, 2, 0))
    early = early_part(place, other_towers, expert_w, far_w, expert_b, far_b, gates)
    hidden_early, gate_early, late_w, gate_late = early
    received, own, hidden_early = lax.optimization_barrier((received, own, hidden_early))

    squeezed = cross_and_compress(here, slot_of_feature[0], received, own, by_row, features, cross_w[0], cross_b, comp_w[0], comp_b)
    opposite = lax.ppermute(squeezed, "tower", swap)
    return mix_experts(place, hidden_early, late_w, gate_early, gate_late, squeezed, opposite)


def solution(mesh):
    return jax.shard_map(
        on_device,
        mesh=mesh,
        in_specs=(
            P("tower", "inner", "groups", None),
            P("tower", "inner", "groups"),
            P("tower", None),
            P("tower", "inner", None, None),
            P("tower", None, None),
            P("tower", None),
            P("tower", None, None),
            P("tower", None),
            P(("groups", "inner"), None),
            P("tower", None, None),
            P("tower", None),
            P(),
        ),
        out_specs=P(("groups", "inner"), None, "tower"),
        check_vma=False,
    )
```

```python
import functools
import math

import jax
import jax.numpy as jnp
from jax import lax
from jax.experimental import pallas as pl
from jax.experimental.pallas import tpu as pltpu
from jax.sharding import PartitionSpec as P

LOW = 256
SHIFT = 8
CHUNKS = 8
PAIR = 1
OWN = 5


def arrange_low(table_low, tab, feature):
    embed, vocab = tab.shape[1], tab.shape[2]
    for part in range(0, vocab // LOW, 2):
        pair = [tab[feature, :, pl.ds((part + n) * LOW, LOW)].astype(jnp.float32) for n in range(2)]
        table_low[pl.ds(part * embed, 2 * embed), :] = jnp.concatenate(pair, axis=0).astype(jnp.bfloat16)


def pool_matched(table_low, high, index, between=None):
    rows, bag = index[0].shape[1], len(index)
    embed = table_low.shape[0] // high
    total = None
    for first in range(0, bag, PAIR):
        ids = jnp.concatenate(index[first : first + PAIR], axis=1)
        width = ids.shape[1]
        upper, lower = jnp.broadcast_to(ids >> SHIFT, (embed, width)), ids & (LOW - 1)
        level = lax.broadcasted_iota(jnp.int32, (LOW, width), 0)
        chosen = (level == lower).astype(jnp.float32).astype(jnp.bfloat16)
        found = jnp.dot(table_low[...], chosen, preferred_element_type=jnp.float32)
        picked = jnp.zeros((embed, width), jnp.float32)
        for part in range(high):
            picked = jnp.where(upper == part, found[part * embed : (part + 1) * embed], picked)
            if between is not None:
                between()
        for j in range(width // rows):
            piece = picked[:, j * rows : (j + 1) * rows]
            total = piece if total is None else total + piece
    return total


def pool_kernel(by_row, tile, groups, row_count, *refs):
    me_ref, ids_hbm, len_hbm, tab_hbm, out_ref, ids_ref, len_ref, shown, tab, table_low, sem = refs[:11]
    features, embed, vocab = tab.shape
    bag, samples = ids_ref.shape[1], ids_ref.shape[2]
    dests = samples // row_count
    high = vocab // LOW
    me = me_ref[0]
    copies = [pltpu.make_async_copy(ids_hbm, ids_ref, sem.at[0]), pltpu.make_async_copy(len_hbm, len_ref, sem.at[1])]
    for copy in copies:
        copy.start()
    parts = []
    if by_row:
        row_ref, pooled, sem_ids = refs[11:14]
        addresses = refs[14:]
        width = vocab // CHUNKS
        for c in range(CHUNKS):
            where = (pl.ds(0, by_row), slice(None), pl.ds(c * width, width))
            parts.append(pltpu.make_async_copy(tab_hbm.at[where], tab.at[where], sem.at[3 + c]))
            parts[-1].start()
    others = pl.ds(by_row, features - by_row)
    rest_copy = pltpu.make_async_copy(tab_hbm.at[others], tab.at[others], sem.at[2])
    if not by_row:
        rest_copy.start()
    for copy in copies:
        copy.wait()
    for f in range(features):
        for j in range(bag):
            shown[f * bag + j] = jnp.where(j < len_ref[pl.ds(f, 1), :], ids_ref[f, pl.ds(j, 1), :], vocab)
    if by_row:
        moves = [pltpu.make_async_copy(shown.at[n, 0], addresses[n], sem_ids.at[n]) for n in range(by_row * bag)]
        for move in moves:
            move.start()
        row_ref[pl.ds(vocab, 8), :] = jnp.zeros((8, 128), jnp.float32)
        square = [lax.broadcasted_iota(jnp.int32, (LOW, LOW), axis) for axis in range(2)]
        unit = (square[0] == square[1]).astype(jnp.float32).astype(jnp.bfloat16)
        blank = jnp.zeros((128 - by_row * embed, LOW), jnp.float32)

        def build(block, carry, first):
            start = pl.multiple_of(first + block * 2 * LOW, 2 * LOW)
            both = []
            for n in range(2):
                both += [tab[f, :, pl.ds(start + n * LOW, LOW)].astype(jnp.float32) for f in range(by_row)] + [blank]
            columns = jnp.concatenate(both, axis=0).astype(jnp.bfloat16)
            turned = lax.dot_general(unit, columns, (((1,), (1,)), ((), ())), preferred_element_type=jnp.float32)
            row_ref[pl.ds(start, LOW), :] = turned[:, :128]
            row_ref[pl.ds(start + LOW, LOW), :] = turned[:, 128:]
            return carry

        for c in range(CHUNKS):
            parts[c].wait()
            if c == CHUNKS // 2 - 1:
                rest_copy.start()
            lax.fori_loop(0, width // (2 * LOW), functools.partial(build, first=c * width), 0, unroll=4)
        for move in moves:
            move.wait()
    rest_copy.wait()
    lane = lax.broadcasted_iota(jnp.int32, (1, 128), 1)

    def other(block):
        dest = me + 1 + block
        return jnp.where(dest >= dests, dest - dests, dest)

    def lookups(group):
        eighths = row_count // 8
        row = pl.multiple_of(other(group // eighths) * row_count + group % eighths * 8, 8)
        for u in range(8):
            line = None
            for f in range(by_row):
                found = [row_ref[pl.ds(addresses[f * bag + j][row + u], 1), :] for j in range(bag)]
                total = found[0]
                for item in found[1:]:
                    total = total + item
                line = total if line is None else jnp.where(lane < embed * f, line, total)
                yield
            pooled[pl.ds(row + u, 1), :] = line

    last = (dests - 1) * row_count // 8 - 1
    tiles = samples // tile

    def step(i, carry):
        feature, t = by_row + i // tiles, i % tiles
        pl.when(t == 0)(functools.partial(arrange_low, table_low, tab, feature))
        work = (item for g in range(groups) for item in lookups(jnp.minimum(i * groups + g, last)))
        wanted = groups * 8 * by_row
        count = [0, 0]

        def between():
            count[0] += 1
            while count[1] * (bag // PAIR) * high < count[0] * wanted:
                next(work, None)
                count[1] += 1

        span = pl.ds(pl.multiple_of(t * tile, tile), tile)
        index = [shown[feature * bag + j, :, span] for j in range(bag)]
        total = pool_matched(table_low, high, index, between)
        for block in range(tile // row_count):
            piece = total[:, block * row_count : (block + 1) * row_count]
            out_ref[t * (tile // row_count) + block, feature] = piece.astype(jnp.bfloat16)
        for _ in work:
            pass
        return carry

    steps = (features - by_row) * tiles
    lax.fori_loop(0, steps, step, 0)
    if by_row:

        def rest(group, carry):
            for _ in lookups(group):
                pass
            return carry

        lax.fori_loop(min(steps * groups, last + 1), last + 1, rest, 0)
    if by_row:
        out_ref[me, pl.ds(0, by_row)] = jnp.zeros((by_row, embed, row_count), jnp.bfloat16)

        def finish(block, carry):
            dest = other(block)
            turned = pooled[pl.ds(pl.multiple_of(dest * row_count, row_count), row_count), :].T
            for f in range(by_row):
                out_ref[dest, f] = turned[f * embed : (f + 1) * embed].astype(jnp.bfloat16)
            return carry

        lax.fori_loop(0, dests - 1, finish, 0, unroll=True)


def row_features(features, embed):
    return min(128 // embed, features * 5 // 8)


def pool_features(place, table, ids, lengths, inner_size):
    features, embed, vocab = table.shape
    bag, samples = ids.shape[1], ids.shape[2]
    row_count = samples // inner_size
    tile = row_count * max(1, min(samples, 1024) // row_count)
    by_row = row_features(features, embed)
    steps = (features - by_row) * (samples // tile)
    groups = (samples - row_count) // 8 // steps if by_row else 0
    hbm = pl.BlockSpec(memory_space=pltpu.HBM)
    scratch = [
        pltpu.VMEM(ids.shape, jnp.int32),
        pltpu.VMEM(lengths.shape, jnp.int32),
        pltpu.VMEM((features * bag, 1, samples), jnp.int32),
        pltpu.VMEM(table.shape, jnp.bfloat16),
        pltpu.VMEM((vocab // LOW * embed, LOW), jnp.bfloat16),
        pltpu.SemaphoreType.DMA((3 + CHUNKS,)),
    ]
    if by_row:
        scratch += [
            pltpu.VMEM((vocab + 8, 128), jnp.float32),
            pltpu.VMEM((samples, 128), jnp.float32),
            pltpu.SemaphoreType.DMA((by_row * bag,)),
        ] + [pltpu.SMEM((samples,), jnp.int32)] * (by_row * bag)
    return pl.pallas_call(
        functools.partial(pool_kernel, by_row, tile, groups, row_count),
        out_shape=pltpu.HBM((inner_size, features, embed, row_count), jnp.bfloat16),
        in_specs=[pl.BlockSpec(memory_space=pltpu.SMEM), hbm, hbm, hbm],
        out_specs=pl.BlockSpec(memory_space=pltpu.VMEM),
        scratch_shapes=scratch,
        compiler_params=pltpu.CompilerParams(vmem_limit_bytes=32 * 2**20),
        name="pool_features",
    )(place, *(pltpu.with_memory_space_constraint(x, pltpu.HBM) for x in (ids, lengths, table)))


def own_kernel(me_ref, ids_ref, len_ref, tab_ref, out_ref, *lows):
    together, vocab = len(lows), tab_ref.shape[2]
    for f, table_low in enumerate(lows):
        arrange_low(table_low, tab_ref, f)
        length = len_ref[pl.ds(pl.program_id(0) * together + f, 1), :]
        index = [jnp.where(j < length, ids_ref[f, pl.ds(j, 1), :], vocab) for j in range(ids_ref.shape[1])]
        out_ref[f] = pool_matched(table_low, vocab // LOW, index).astype(jnp.bfloat16)


def pool_own(place, table, ids, lengths, inner_size):
    all_features, embed, vocab = table.shape
    features = row_features(all_features, embed)
    bag, samples = ids.shape[1], ids.shape[2]
    rows = samples // inner_size
    together = math.gcd(features, OWN)
    return pl.pallas_call(
        own_kernel,
        out_shape=jax.ShapeDtypeStruct((features, embed, rows), jnp.bfloat16),
        grid_spec=pltpu.PrefetchScalarGridSpec(
            num_scalar_prefetch=1,
            grid=(features // together,),
            in_specs=[
                pl.BlockSpec((together, bag, rows), lambda f, me: (f, 0, me[0])),
                pl.BlockSpec((all_features, rows), lambda f, me: (0, me[0])),
                pl.BlockSpec((together, embed, vocab), lambda f, me: (f, 0, 0)),
            ],
            out_specs=pl.BlockSpec((together, embed, rows), lambda f, me: (f, 0, 0)),
            scratch_shapes=[pltpu.VMEM((vocab // LOW * embed, LOW), jnp.bfloat16)] * together,
        ),
        compiler_params=pltpu.CompilerParams(vmem_limit_bytes=16 * 2**20),
        cost_estimate=pl.CostEstimate(
            flops=2 * features * bag * rows * vocab * embed, bytes_accessed=2 * table.size, transcendentals=0
        ),
        name="pool_own",
    )(place, *(pltpu.with_memory_space_constraint(x, pltpu.HBM) for x in (ids, lengths, table)))


def early_kernel(known, tower_ref, other_ref, own_hbm, far_hbm, own_bias_ref, far_bias_ref, gate_ref, *refs):
    early_ref, gate_early_ref, late_ref, gate_late_ref, weights, sem = refs
    tower = tower_ref[0]
    half, experts_in, columns = own_hbm.shape[0], weights.shape[1], weights.shape[2]
    span = pl.ds(pl.multiple_of(tower * columns, columns), columns)
    copies = []
    for n, (source, place) in enumerate([(own_hbm, tower), (far_hbm, 1 - tower)]):
        for e in range(half):
            copies.append(
                pltpu.make_async_copy(source.at[e, :, span], weights.at[place * half + e], sem.at[n * half + e])
            )
            copies[-1].start()
    tasks, experts, depth = gate_ref.shape
    gates = gate_ref[...].astype(jnp.float32).reshape(tasks * experts, depth).astype(jnp.bfloat16)
    gate_early_ref[...] = lax.dot_general(
        other_ref[...], gates[:, :known], (((1,), (1,)), ((), ())), preferred_element_type=jnp.float32
    )
    gate_late_ref[...] = gates[:, known:]
    for n, (bias, place) in enumerate([(own_bias_ref, tower), (far_bias_ref, 1 - tower)]):
        for e in range(half):
            copies[n * half + e].wait()
            at = place * half + e
            found = jnp.dot(other_ref[...], weights[at, pl.ds(0, known), :], preferred_element_type=jnp.float32)
            early_ref[at] = found + bias[pl.ds(e, 1), span]
            late_ref[at] = weights[at, pl.ds(known, experts_in - known), :]


def early_part(tower, other, own_w, far_w, own_b, far_b, gates):
    half, depth, hidden = own_w.shape
    rows, known = other.shape
    columns = hidden // 2
    vmem, hbm = pl.BlockSpec(memory_space=pltpu.VMEM), pl.BlockSpec(memory_space=pltpu.HBM)
    count = gates.shape[0] * gates.shape[1]
    far = lambda x: pltpu.with_memory_space_constraint(x, pltpu.HBM)
    return pl.pallas_call(
        functools.partial(early_kernel, known),
        out_shape=(
            jax.ShapeDtypeStruct((2 * half, rows, columns), jnp.float32),
            jax.ShapeDtypeStruct((rows, count), jnp.float32),
            jax.ShapeDtypeStruct((2 * half, depth - known, columns), jnp.bfloat16),
            jax.ShapeDtypeStruct((count, depth - known), jnp.bfloat16),
        ),
        in_specs=[pl.BlockSpec(memory_space=pltpu.SMEM), vmem, hbm, hbm, vmem, vmem, vmem],
        out_specs=(vmem,) * 4,
        scratch_shapes=[pltpu.VMEM((2 * half, depth, columns), jnp.bfloat16), pltpu.SemaphoreType.DMA((2 * half,))],
        compiler_params=pltpu.CompilerParams(vmem_limit_bytes=16 * 2**20),
        cost_estimate=pl.CostEstimate(
            flops=4 * half * rows * known * columns,
            bytes_accessed=4 * half * depth * columns,
            transcendentals=0,
        ),
        name="early_part",
    )(tower, other, far(own_w), far_w, own_b, far_b, gates)


def cross_kernel(each, by_row, me_ref, slot_ref, rec_ref, own_ref, w_hbm, bias_ref, comp_ref, comp_bias_ref, *refs):
    out_ref, first_t, first, w_ref, sums, sem = refs
    slots, embed, rows = rec_ref.shape
    width, blocks = w_ref.shape[1], sem.shape[0]
    step = width // blocks
    spans = [pl.ds(n * step, step) for n in range(blocks)]
    copies = [pltpu.make_async_copy(w_hbm.at[span], w_ref.at[span], sem.at[n]) for n, span in enumerate(spans)]
    for copy in copies:
        copy.start()
    for f in range(slots):
        first_t[slot_ref[f]] = rec_ref[f].astype(jnp.float32)
    for f in range(by_row):
        first_t[slot_ref[me_ref[0] * each + f]] = own_ref[f].astype(jnp.float32)
    first[...] = first_t[...].reshape(width, rows).T.astype(jnp.bfloat16)
    crossed = bias_ref[...]
    for n, span in enumerate(spans):
        copies[n].wait()
        crossed = crossed + jnp.dot(first[:, span], w_ref[span, :], preferred_element_type=jnp.float32)
        if n + 1 < blocks:
            sums[...] = crossed
            crossed = sums[...]
    total = jnp.zeros((rows, comp_ref.shape[0]), jnp.float32) + comp_bias_ref[...]
    for n, span in enumerate(spans):
        base = first[:, span].astype(jnp.float32)
        second = (base * crossed[:, n * step : (n + 1) * step] + base).astype(jnp.bfloat16)
        total = total + lax.dot_general(
            second, comp_ref[:, span], (((1,), (1,)), ((), ())), preferred_element_type=jnp.float32
        )
    out_ref[...] = total.astype(jnp.bfloat16)


def cross_and_compress(place, slots, received, own, by_row, each, cross_w, cross_b, comp_w, comp_b):
    slot_total, embed, rows = received.shape
    width = cross_w.shape[0]
    vmem, smem = pl.BlockSpec(memory_space=pltpu.VMEM), pl.BlockSpec(memory_space=pltpu.SMEM)
    return pl.pallas_call(
        functools.partial(cross_kernel, each, by_row),
        out_shape=jax.ShapeDtypeStruct((rows, comp_w.shape[1]), jnp.bfloat16),
        in_specs=[smem, smem, vmem, vmem, pl.BlockSpec(memory_space=pltpu.HBM), vmem, vmem, vmem],
        out_specs=vmem,
        scratch_shapes=[
            pltpu.VMEM((slot_total, embed, rows), jnp.float32),
            pltpu.VMEM((rows, width), jnp.bfloat16),
            pltpu.VMEM(cross_w.shape, jnp.bfloat16),
            pltpu.VMEM((rows, width), jnp.float32),
            pltpu.SemaphoreType.DMA((width // 256,)),
        ],
        compiler_params=pltpu.CompilerParams(vmem_limit_bytes=16 * 2**20),
        name="cross_and_compress",
    )(place, slots, received, own, pltpu.with_memory_space_constraint(cross_w, pltpu.HBM), cross_b, comp_w.T, comp_b)


def mix_kernel(tower_ref, early_ref, late_ref, gate_early_ref, gate_late_ref, own_ref, far_ref, out_ref, hidden_ref, lines_ref):
    experts, rows, columns = early_ref.shape
    tasks = gate_early_ref.shape[1] // experts
    own, far = own_ref[...], far_ref[...]
    lead = tower_ref[0] == 0
    squeezed = jnp.concatenate([jnp.where(lead, own, far), jnp.where(lead, far, own)], axis=1)
    logits = gate_early_ref[...] + lax.dot_general(
        squeezed, gate_late_ref[...], (((1,), (1,)), ((), ())), preferred_element_type=jnp.float32
    )
    weights = jnp.exp(logits)
    probs = []
    for k in range(tasks):
        mine = weights[:, k * experts : (k + 1) * experts]
        probs.append(mine / jnp.sum(mine, axis=1, keepdims=True))
    for e in range(experts):
        hidden = early_ref[e] + jnp.dot(squeezed, late_ref[e], preferred_element_type=jnp.float32)
        hidden_ref[e] = jnp.maximum(hidden, 0.0).astype(jnp.bfloat16).astype(jnp.float32)
    step = math.gcd(rows, 32)
    for first in range(0, rows, step):
        totals = [0.0] * tasks
        for e in range(experts):
            hidden = hidden_ref[e, pl.ds(first, step), :]
            for k in range(tasks):
                totals[k] = totals[k] + probs[k][first : first + step, e : e + 1] * hidden
        for c in range(columns // 128):
            for k in range(tasks):
                lines_ref[c, pl.ds(first * tasks + k, step, stride=tasks), :] = totals[k][:, c * 128 : (c + 1) * 128]
            lines = lines_ref[c, pl.ds(first * tasks, step * tasks), :].reshape(step, tasks, 128)
            out_ref[pl.ds(first, step), :, pl.ds(c * 128, 128)] = lines.astype(jnp.bfloat16)


def mix_experts(tower, early, late, gate_early, gate_late, own, far):
    experts, rows, columns = early.shape
    tasks = gate_early.shape[1] // experts
    vmem = pl.BlockSpec(memory_space=pltpu.VMEM)
    return pl.pallas_call(
        mix_kernel,
        out_shape=jax.ShapeDtypeStruct((rows, tasks, columns), jnp.bfloat16),
        in_specs=[pl.BlockSpec(memory_space=pltpu.SMEM)] + [vmem] * 6,
        out_specs=vmem,
        scratch_shapes=[
            pltpu.VMEM((experts, rows, columns), jnp.float32),
            pltpu.VMEM((columns // 128, rows * tasks, 128), jnp.float32),
        ],
        compiler_params=pltpu.CompilerParams(vmem_limit_bytes=16 * 2**20),
        name="mix_experts",
    )(tower, early, late, gate_early, gate_late, own, far)


def on_device(
    ids,
    bag_len,
    slot_of_feature,
    tables,
    cross_w,
    cross_b,
    comp_w,
    comp_b,
    other_towers,
    expert_w,
    expert_b,
    gate_w,
):
    inner_size = lax.axis_size("inner")
    tower_size = lax.axis_size("tower")
    tower = lax.axis_index("tower")
    swap = [(n, (n + 1) % tower_size) for n in range(tower_size)]

    far_w = lax.ppermute(expert_w, "tower", swap)
    far_b = lax.ppermute(expert_b, "tower", swap)

    here = lax.axis_index("inner").reshape(1)
    tables_t, ids_t = jnp.transpose(tables[0], (0, 2, 1)), jnp.transpose(ids[0], (0, 2, 1))
    pooled = pool_features(here, tables_t, ids_t, bag_len[0], inner_size)
    dests, features, embed, rows = pooled.shape
    pooled = pooled.reshape(dests, features * embed, rows)
    received = lax.all_to_all(pooled, "inner", split_axis=0, concat_axis=0, tiled=True)
    received = received.reshape(dests * features, embed, rows)

    by_row = row_features(features, embed)
    own = pool_own(here, tables_t, ids_t, bag_len[0], inner_size) if by_row else received[:1]
    place = tower.reshape(1)
    gates = jnp.transpose(gate_w, (1, 2, 0))
    early = early_part(place, other_towers, expert_w, far_w, expert_b, far_b, gates)
    hidden_early, gate_early, late_w, gate_late = early
    received, own, hidden_early = lax.optimization_barrier((received, own, hidden_early))

    squeezed = cross_and_compress(here, slot_of_feature[0], received, own, by_row, features, cross_w[0], cross_b, comp_w[0], comp_b)
    opposite = lax.ppermute(squeezed, "tower", swap)
    return mix_experts(place, hidden_early, late_w, gate_early, gate_late, squeezed, opposite)


def solution(mesh):
    return jax.shard_map(
        on_device,
        mesh=mesh,
        in_specs=(
            P("tower", "inner", "groups", None),
            P("tower", "inner", "groups"),
            P("tower", None),
            P("tower", "inner", None, None),
            P("tower", None, None),
            P("tower", None),
            P("tower", None, None),
            P("tower", None),
            P(("groups", "inner"), None),
            P("tower", None, None),
            P("tower", None),
            P(),
        ),
        out_specs=P(("groups", "inner"), None, "tower"),
        check_vma=False,
    )
```

```python
import functools
import math

import jax
import jax.numpy as jnp
from jax import lax
from jax.experimental import pallas as pl
from jax.experimental.pallas import tpu as pltpu
from jax.sharding import PartitionSpec as P

LOW = 256
SHIFT = 8
CHUNKS = 4
PAIR = 1
OWN = 5


def arrange_low(table_low, tab, feature):
    embed, vocab = tab.shape[1], tab.shape[2]
    for part in range(0, vocab // LOW, 2):
        pair = [tab[feature, :, pl.ds((part + n) * LOW, LOW)].astype(jnp.float32) for n in range(2)]
        table_low[pl.ds(part * embed, 2 * embed), :] = jnp.concatenate(pair, axis=0).astype(jnp.bfloat16)


def pool_matched(table_low, high, index, between=None):
    rows, bag = index[0].shape[1], len(index)
    embed = table_low.shape[0] // high
    total = None
    for first in range(0, bag, PAIR):
        ids = jnp.concatenate(index[first : first + PAIR], axis=1)
        width = ids.shape[1]
        upper, lower = jnp.broadcast_to(ids >> SHIFT, (embed, width)), ids & (LOW - 1)
        level = lax.broadcasted_iota(jnp.int32, (LOW, width), 0)
        chosen = (level == lower).astype(jnp.float32).astype(jnp.bfloat16)
        found = jnp.dot(table_low[...], chosen, preferred_element_type=jnp.float32)
        picked = jnp.zeros((embed, width), jnp.float32)
        for part in range(high):
            picked = jnp.where(upper == part, found[part * embed : (part + 1) * embed], picked)
            if between is not None:
                between()
        for j in range(width // rows):
            piece = picked[:, j * rows : (j + 1) * rows]
            total = piece if total is None else total + piece
    return total


def pool_kernel(by_row, tile, groups, row_count, *refs):
    me_ref, ids_hbm, len_hbm, tab_hbm, out_ref, ids_ref, len_ref, shown, tab, table_low, sem = refs[:11]
    features, embed, vocab = tab.shape
    bag, samples = ids_ref.shape[1], ids_ref.shape[2]
    dests = samples // row_count
    high = vocab // LOW
    me = me_ref[0]
    copies = [pltpu.make_async_copy(ids_hbm, ids_ref, sem.at[0]), pltpu.make_async_copy(len_hbm, len_ref, sem.at[1])]
    for copy in copies:
        copy.start()
    parts = []
    if by_row:
        row_ref, pooled, sem_ids = refs[11:14]
        addresses = refs[14:]
        width = vocab // CHUNKS
        for c in range(CHUNKS):
            where = (pl.ds(0, by_row), slice(None), pl.ds(c * width, width))
            parts.append(pltpu.make_async_copy(tab_hbm.at[where], tab.at[where], sem.at[3 + c]))
            parts[-1].start()
    others = pl.ds(by_row, features - by_row)
    rest_copy = pltpu.make_async_copy(tab_hbm.at[others], tab.at[others], sem.at[2])
    if not by_row:
        rest_copy.start()
    for copy in copies:
        copy.wait()
    for f in range(features):
        for j in range(bag):
            shown[f * bag + j] = jnp.where(j < len_ref[pl.ds(f, 1), :], ids_ref[f, pl.ds(j, 1), :], vocab)
    if by_row:
        moves = [pltpu.make_async_copy(shown.at[n, 0], addresses[n], sem_ids.at[n]) for n in range(by_row * bag)]
        for move in moves:
            move.start()
        row_ref[pl.ds(vocab, 8), :] = jnp.zeros((8, 128), jnp.float32)
        square = [lax.broadcasted_iota(jnp.int32, (LOW, LOW), axis) for axis in range(2)]
        unit = (square[0] == square[1]).astype(jnp.float32).astype(jnp.bfloat16)
        blank = jnp.zeros((128 - by_row * embed, LOW), jnp.float32)

        def build(block, carry, first):
            start = pl.multiple_of(first + block * 2 * LOW, 2 * LOW)
            both = []
            for n in range(2):
                both += [tab[f, :, pl.ds(start + n * LOW, LOW)].astype(jnp.float32) for f in range(by_row)] + [blank]
            columns = jnp.concatenate(both, axis=0).astype(jnp.bfloat16)
            turned = lax.dot_general(unit, columns, (((1,), (1,)), ((), ())), preferred_element_type=jnp.float32)
            row_ref[pl.ds(start, LOW), :] = turned[:, :128]
            row_ref[pl.ds(start + LOW, LOW), :] = turned[:, 128:]
            return carry

        for c in range(CHUNKS):
            parts[c].wait()
            if c == CHUNKS // 2 - 1:
                rest_copy.start()
            lax.fori_loop(0, width // (2 * LOW), functools.partial(build, first=c * width), 0, unroll=8)
        for move in moves:
            move.wait()
    rest_copy.wait()
    lane = lax.broadcasted_iota(jnp.int32, (1, 128), 1)

    def other(block):
        dest = me + 1 + block
        return jnp.where(dest >= dests, dest - dests, dest)

    def lookups(group):
        eighths = row_count // 8
        row = pl.multiple_of(other(group // eighths) * row_count + group % eighths * 8, 8)
        for u in range(8):
            line = None
            for f in range(by_row):
                found = [row_ref[pl.ds(addresses[f * bag + j][row + u], 1), :] for j in range(bag)]
                total = found[0]
                for item in found[1:]:
                    total = total + item
                line = total if line is None else jnp.where(lane < embed * f, line, total)
                yield
            pooled[pl.ds(row + u, 1), :] = line

    last = (dests - 1) * row_count // 8 - 1
    tiles = samples // tile

    def step(i, carry):
        feature, t = by_row + i // tiles, i % tiles
        pl.when(t == 0)(functools.partial(arrange_low, table_low, tab, feature))
        work = (item for g in range(groups) for item in lookups(jnp.minimum(i * groups + g, last)))
        wanted = groups * 8 * by_row
        count = [0, 0]

        def between():
            count[0] += 1
            while count[1] * (bag // PAIR) * high < count[0] * wanted:
                next(work, None)
                count[1] += 1

        span = pl.ds(pl.multiple_of(t * tile, tile), tile)
        index = [shown[feature * bag + j, :, span] for j in range(bag)]
        total = pool_matched(table_low, high, index, between)
        for block in range(tile // row_count):
            piece = total[:, block * row_count : (block + 1) * row_count]
            out_ref[t * (tile // row_count) + block, feature] = piece.astype(jnp.bfloat16)
        for _ in work:
            pass
        return carry

    steps = (features - by_row) * tiles
    lax.fori_loop(0, steps, step, 0)
    if by_row:

        def rest(group, carry):
            for _ in lookups(group):
                pass
            return carry

        lax.fori_loop(min(steps * groups, last + 1), last + 1, rest, 0)
    if by_row:
        out_ref[me, pl.ds(0, by_row)] = jnp.zeros((by_row, embed, row_count), jnp.bfloat16)

        def finish(block, carry):
            dest = other(block)
            turned = pooled[pl.ds(pl.multiple_of(dest * row_count, row_count), row_count), :].T
            for f in range(by_row):
                out_ref[dest, f] = turned[f * embed : (f + 1) * embed].astype(jnp.bfloat16)
            return carry

        lax.fori_loop(0, dests - 1, finish, 0, unroll=True)


def row_features(features, embed):
    return min(128 // embed, features * 5 // 8)


def pool_features(place, table, ids, lengths, inner_size):
    features, embed, vocab = table.shape
    bag, samples = ids.shape[1], ids.shape[2]
    row_count = samples // inner_size
    tile = row_count * max(1, min(samples, 1024) // row_count)
    by_row = row_features(features, embed)
    steps = (features - by_row) * (samples // tile)
    groups = (samples - row_count) // 8 // steps if by_row else 0
    hbm = pl.BlockSpec(memory_space=pltpu.HBM)
    scratch = [
        pltpu.VMEM(ids.shape, jnp.int32),
        pltpu.VMEM(lengths.shape, jnp.int32),
        pltpu.VMEM((features * bag, 1, samples), jnp.int32),
        pltpu.VMEM(table.shape, jnp.bfloat16),
        pltpu.VMEM((vocab // LOW * embed, LOW), jnp.bfloat16),
        pltpu.SemaphoreType.DMA((3 + CHUNKS,)),
    ]
    if by_row:
        scratch += [
            pltpu.VMEM((vocab + 8, 128), jnp.float32),
            pltpu.VMEM((samples, 128), jnp.float32),
            pltpu.SemaphoreType.DMA((by_row * bag,)),
        ] + [pltpu.SMEM((samples,), jnp.int32)] * (by_row * bag)
    return pl.pallas_call(
        functools.partial(pool_kernel, by_row, tile, groups, row_count),
        out_shape=pltpu.HBM((inner_size, features, embed, row_count), jnp.bfloat16),
        in_specs=[pl.BlockSpec(memory_space=pltpu.SMEM), hbm, hbm, hbm],
        out_specs=pl.BlockSpec(memory_space=pltpu.VMEM),
        scratch_shapes=scratch,
        compiler_params=pltpu.CompilerParams(vmem_limit_bytes=32 * 2**20),
        name="pool_features",
    )(place, *(pltpu.with_memory_space_constraint(x, pltpu.HBM) for x in (ids, lengths, table)))


def own_kernel(me_ref, ids_ref, len_ref, tab_ref, out_ref, *lows):
    together, vocab = len(lows), tab_ref.shape[2]
    for f, table_low in enumerate(lows):
        arrange_low(table_low, tab_ref, f)
        length = len_ref[pl.ds(pl.program_id(0) * together + f, 1), :]
        index = [jnp.where(j < length, ids_ref[f, pl.ds(j, 1), :], vocab) for j in range(ids_ref.shape[1])]
        out_ref[f] = pool_matched(table_low, vocab // LOW, index).astype(jnp.bfloat16)


def pool_own(place, table, ids, lengths, inner_size):
    all_features, embed, vocab = table.shape
    features = row_features(all_features, embed)
    bag, samples = ids.shape[1], ids.shape[2]
    rows = samples // inner_size
    together = math.gcd(features, OWN)
    return pl.pallas_call(
        own_kernel,
        out_shape=jax.ShapeDtypeStruct((features, embed, rows), jnp.bfloat16),
        grid_spec=pltpu.PrefetchScalarGridSpec(
            num_scalar_prefetch=1,
            grid=(features // together,),
            in_specs=[
                pl.BlockSpec((together, bag, rows), lambda f, me: (f, 0, me[0])),
                pl.BlockSpec((all_features, rows), lambda f, me: (0, me[0])),
                pl.BlockSpec((together, embed, vocab), lambda f, me: (f, 0, 0)),
            ],
            out_specs=pl.BlockSpec((together, embed, rows), lambda f, me: (f, 0, 0)),
            scratch_shapes=[pltpu.VMEM((vocab // LOW * embed, LOW), jnp.bfloat16)] * together,
        ),
        compiler_params=pltpu.CompilerParams(vmem_limit_bytes=16 * 2**20),
        cost_estimate=pl.CostEstimate(
            flops=2 * features * bag * rows * vocab * embed, bytes_accessed=2 * table.size, transcendentals=0
        ),
        name="pool_own",
    )(place, *(pltpu.with_memory_space_constraint(x, pltpu.HBM) for x in (ids, lengths, table)))


def early_kernel(known, tower_ref, other_ref, own_hbm, far_hbm, own_bias_ref, far_bias_ref, gate_ref, *refs):
    early_ref, gate_early_ref, late_ref, gate_late_ref, weights, sem = refs
    tower = tower_ref[0]
    half, experts_in, columns = own_hbm.shape[0], weights.shape[1], weights.shape[2]
    span = pl.ds(pl.multiple_of(tower * columns, columns), columns)
    copies = []
    for n, (source, place) in enumerate([(own_hbm, tower), (far_hbm, 1 - tower)]):
        for e in range(half):
            copies.append(
                pltpu.make_async_copy(source.at[e, :, span], weights.at[place * half + e], sem.at[n * half + e])
            )
            copies[-1].start()
    tasks, experts, depth = gate_ref.shape
    gates = gate_ref[...].astype(jnp.float32).reshape(tasks * experts, depth).astype(jnp.bfloat16)
    gate_early_ref[...] = lax.dot_general(
        other_ref[...], gates[:, :known], (((1,), (1,)), ((), ())), preferred_element_type=jnp.float32
    )
    gate_late_ref[...] = gates[:, known:]
    for n, (bias, place) in enumerate([(own_bias_ref, tower), (far_bias_ref, 1 - tower)]):
        for e in range(half):
            copies[n * half + e].wait()
            at = place * half + e
            found = jnp.dot(other_ref[...], weights[at, pl.ds(0, known), :], preferred_element_type=jnp.float32)
            early_ref[at] = found + bias[pl.ds(e, 1), span]
            late_ref[at] = weights[at, pl.ds(known, experts_in - known), :]


def early_part(tower, other, own_w, far_w, own_b, far_b, gates):
    half, depth, hidden = own_w.shape
    rows, known = other.shape
    columns = hidden // 2
    vmem, hbm = pl.BlockSpec(memory_space=pltpu.VMEM), pl.BlockSpec(memory_space=pltpu.HBM)
    count = gates.shape[0] * gates.shape[1]
    far = lambda x: pltpu.with_memory_space_constraint(x, pltpu.HBM)
    return pl.pallas_call(
        functools.partial(early_kernel, known),
        out_shape=(
            jax.ShapeDtypeStruct((2 * half, rows, columns), jnp.float32),
            jax.ShapeDtypeStruct((rows, count), jnp.float32),
            jax.ShapeDtypeStruct((2 * half, depth - known, columns), jnp.bfloat16),
            jax.ShapeDtypeStruct((count, depth - known), jnp.bfloat16),
        ),
        in_specs=[pl.BlockSpec(memory_space=pltpu.SMEM), vmem, hbm, hbm, vmem, vmem, vmem],
        out_specs=(vmem,) * 4,
        scratch_shapes=[pltpu.VMEM((2 * half, depth, columns), jnp.bfloat16), pltpu.SemaphoreType.DMA((2 * half,))],
        compiler_params=pltpu.CompilerParams(vmem_limit_bytes=16 * 2**20),
        cost_estimate=pl.CostEstimate(
            flops=4 * half * rows * known * columns,
            bytes_accessed=4 * half * depth * columns,
            transcendentals=0,
        ),
        name="early_part",
    )(tower, other, far(own_w), far_w, own_b, far_b, gates)


def cross_kernel(each, by_row, me_ref, slot_ref, rec_ref, own_ref, w_hbm, bias_ref, comp_ref, comp_bias_ref, *refs):
    out_ref, first_t, first, w_ref, sums, sem = refs
    slots, embed, rows = rec_ref.shape
    width, blocks = w_ref.shape[1], sem.shape[0]
    step = width // blocks
    spans = [pl.ds(n * step, step) for n in range(blocks)]
    copies = [pltpu.make_async_copy(w_hbm.at[span], w_ref.at[span], sem.at[n]) for n, span in enumerate(spans)]
    for copy in copies:
        copy.start()
    for f in range(slots):
        first_t[slot_ref[f]] = rec_ref[f].astype(jnp.float32)
    for f in range(by_row):
        first_t[slot_ref[me_ref[0] * each + f]] = own_ref[f].astype(jnp.float32)
    first[...] = first_t[...].reshape(width, rows).T.astype(jnp.bfloat16)
    crossed = bias_ref[...]
    for n, span in enumerate(spans):
        copies[n].wait()
        crossed = crossed + jnp.dot(first[:, span], w_ref[span, :], preferred_element_type=jnp.float32)
        if n + 1 < blocks:
            sums[...] = crossed
            crossed = sums[...]
    total = jnp.zeros((rows, comp_ref.shape[0]), jnp.float32) + comp_bias_ref[...]
    for n, span in enumerate(spans):
        base = first[:, span].astype(jnp.float32)
        second = (base * crossed[:, n * step : (n + 1) * step] + base).astype(jnp.bfloat16)
        total = total + lax.dot_general(
            second, comp_ref[:, span], (((1,), (1,)), ((), ())), preferred_element_type=jnp.float32
        )
    out_ref[...] = total.astype(jnp.bfloat16)


def cross_and_compress(place, slots, received, own, by_row, each, cross_w, cross_b, comp_w, comp_b):
    slot_total, embed, rows = received.shape
    width = cross_w.shape[0]
    vmem, smem = pl.BlockSpec(memory_space=pltpu.VMEM), pl.BlockSpec(memory_space=pltpu.SMEM)
    return pl.pallas_call(
        functools.partial(cross_kernel, each, by_row),
        out_shape=jax.ShapeDtypeStruct((rows, comp_w.shape[1]), jnp.bfloat16),
        in_specs=[smem, smem, vmem, vmem, pl.BlockSpec(memory_space=pltpu.HBM), vmem, vmem, vmem],
        out_specs=vmem,
        scratch_shapes=[
            pltpu.VMEM((slot_total, embed, rows), jnp.float32),
            pltpu.VMEM((rows, width), jnp.bfloat16),
            pltpu.VMEM(cross_w.shape, jnp.bfloat16),
            pltpu.VMEM((rows, width), jnp.float32),
            pltpu.SemaphoreType.DMA((width // 256,)),
        ],
        compiler_params=pltpu.CompilerParams(vmem_limit_bytes=16 * 2**20),
        name="cross_and_compress",
    )(place, slots, received, own, pltpu.with_memory_space_constraint(cross_w, pltpu.HBM), cross_b, comp_w.T, comp_b)


def mix_kernel(tower_ref, early_ref, late_ref, gate_early_ref, gate_late_ref, own_ref, far_ref, out_ref, hidden_ref, lines_ref):
    experts, rows, columns = early_ref.shape
    tasks = gate_early_ref.shape[1] // experts
    own, far = own_ref[...], far_ref[...]
    lead = tower_ref[0] == 0
    squeezed = jnp.concatenate([jnp.where(lead, own, far), jnp.where(lead, far, own)], axis=1)
    logits = gate_early_ref[...] + lax.dot_general(
        squeezed, gate_late_ref[...], (((1,), (1,)), ((), ())), preferred_element_type=jnp.float32
    )
    weights = jnp.exp(logits)
    probs = []
    for k in range(tasks):
        mine = weights[:, k * experts : (k + 1) * experts]
        probs.append(mine / jnp.sum(mine, axis=1, keepdims=True))
    for e in range(experts):
        hidden = early_ref[e] + jnp.dot(squeezed, late_ref[e], preferred_element_type=jnp.float32)
        hidden_ref[e] = jnp.maximum(hidden, 0.0).astype(jnp.bfloat16).astype(jnp.float32)
    step = math.gcd(rows, 32)
    for first in range(0, rows, step):
        totals = [0.0] * tasks
        for e in range(experts):
            hidden = hidden_ref[e, pl.ds(first, step), :]
            for k in range(tasks):
                totals[k] = totals[k] + probs[k][first : first + step, e : e + 1] * hidden
        for c in range(columns // 128):
            for k in range(tasks):
                lines_ref[c, pl.ds(first * tasks + k, step, stride=tasks), :] = totals[k][:, c * 128 : (c + 1) * 128]
            lines = lines_ref[c, pl.ds(first * tasks, step * tasks), :].reshape(step, tasks, 128)
            out_ref[pl.ds(first, step), :, pl.ds(c * 128, 128)] = lines.astype(jnp.bfloat16)


def mix_experts(tower, early, late, gate_early, gate_late, own, far):
    experts, rows, columns = early.shape
    tasks = gate_early.shape[1] // experts
    vmem = pl.BlockSpec(memory_space=pltpu.VMEM)
    return pl.pallas_call(
        mix_kernel,
        out_shape=jax.ShapeDtypeStruct((rows, tasks, columns), jnp.bfloat16),
        in_specs=[pl.BlockSpec(memory_space=pltpu.SMEM)] + [vmem] * 6,
        out_specs=vmem,
        scratch_shapes=[
            pltpu.VMEM((experts, rows, columns), jnp.float32),
            pltpu.VMEM((columns // 128, rows * tasks, 128), jnp.float32),
        ],
        compiler_params=pltpu.CompilerParams(vmem_limit_bytes=16 * 2**20),
        name="mix_experts",
    )(tower, early, late, gate_early, gate_late, own, far)


def on_device(
    ids,
    bag_len,
    slot_of_feature,
    tables,
    cross_w,
    cross_b,
    comp_w,
    comp_b,
    other_towers,
    expert_w,
    expert_b,
    gate_w,
):
    inner_size = lax.axis_size("inner")
    tower_size = lax.axis_size("tower")
    tower = lax.axis_index("tower")
    swap = [(n, (n + 1) % tower_size) for n in range(tower_size)]

    far_w = lax.ppermute(expert_w, "tower", swap)
    far_b = lax.ppermute(expert_b, "tower", swap)

    here = lax.axis_index("inner").reshape(1)
    tables_t, ids_t = jnp.transpose(tables[0], (0, 2, 1)), jnp.transpose(ids[0], (0, 2, 1))
    pooled = pool_features(here, tables_t, ids_t, bag_len[0], inner_size)
    dests, features, embed, rows = pooled.shape
    pooled = pooled.reshape(dests, features * embed, rows)
    received = lax.all_to_all(pooled, "inner", split_axis=0, concat_axis=0, tiled=True)
    received = received.reshape(dests * features, embed, rows)

    by_row = row_features(features, embed)
    own = pool_own(here, tables_t, ids_t, bag_len[0], inner_size) if by_row else received[:1]
    place = tower.reshape(1)
    gates = jnp.transpose(gate_w, (1, 2, 0))
    early = early_part(place, other_towers, expert_w, far_w, expert_b, far_b, gates)
    hidden_early, gate_early, late_w, gate_late = early
    received, own, hidden_early = lax.optimization_barrier((received, own, hidden_early))

    squeezed = cross_and_compress(here, slot_of_feature[0], received, own, by_row, features, cross_w[0], cross_b, comp_w[0], comp_b)
    opposite = lax.ppermute(squeezed, "tower", swap)
    return mix_experts(place, hidden_early, late_w, gate_early, gate_late, squeezed, opposite)


def solution(mesh):
    return jax.shard_map(
        on_device,
        mesh=mesh,
        in_specs=(
            P("tower", "inner", "groups", None),
            P("tower", "inner", "groups"),
            P("tower", None),
            P("tower", "inner", None, None),
            P("tower", None, None),
            P("tower", None),
            P("tower", None, None),
            P("tower", None),
            P(("groups", "inner"), None),
            P("tower", None, None),
            P("tower", None),
            P(),
        ),
        out_specs=P(("groups", "inner"), None, "tower"),
        check_vma=False,
    )
```

```python
import functools
import math

import jax
import jax.numpy as jnp
from jax import lax
from jax.experimental import pallas as pl
from jax.experimental.pallas import tpu as pltpu
from jax.sharding import PartitionSpec as P

LOW = 256
SHIFT = 8
CHUNKS = 4
PAIR = 1
OWN = 5


def arrange_low(table_low, tab, feature):
    embed, vocab = tab.shape[1], tab.shape[2]
    for part in range(0, vocab // LOW, 2):
        pair = [tab[feature, :, pl.ds((part + n) * LOW, LOW)].astype(jnp.float32) for n in range(2)]
        table_low[pl.ds(part * embed, 2 * embed), :] = jnp.concatenate(pair, axis=0).astype(jnp.bfloat16)


def pool_matched(table_low, high, index, between=None):
    rows, bag = index[0].shape[1], len(index)
    embed = table_low.shape[0] // high
    total = None
    for first in range(0, bag, PAIR):
        ids = jnp.concatenate(index[first : first + PAIR], axis=1)
        width = ids.shape[1]
        upper, lower = jnp.broadcast_to(ids >> SHIFT, (embed, width)), ids & (LOW - 1)
        level = lax.broadcasted_iota(jnp.int32, (LOW, width), 0)
        chosen = (level == lower).astype(jnp.float32).astype(jnp.bfloat16)
        found = jnp.dot(table_low[...], chosen, preferred_element_type=jnp.float32)
        picked = jnp.zeros((embed, width), jnp.float32)
        for part in range(high):
            picked = jnp.where(upper == part, found[part * embed : (part + 1) * embed], picked)
            if between is not None:
                between()
        for j in range(width // rows):
            piece = picked[:, j * rows : (j + 1) * rows]
            total = piece if total is None else total + piece
    return total


def pool_kernel(by_row, tile, groups, row_count, *refs):
    me_ref, ids_hbm, len_hbm, tab_hbm, out_ref, ids_ref, len_ref, shown, tab, table_low, sem = refs[:11]
    features, embed, vocab = tab.shape
    bag, samples = ids_ref.shape[1], ids_ref.shape[2]
    dests = samples // row_count
    high = vocab // LOW
    me = me_ref[0]
    copies = [pltpu.make_async_copy(ids_hbm, ids_ref, sem.at[0]), pltpu.make_async_copy(len_hbm, len_ref, sem.at[1])]
    for copy in copies:
        copy.start()
    parts = []
    if by_row:
        row_ref, pooled, sem_ids = refs[11:14]
        addresses = refs[14:]
        width = vocab // CHUNKS
        for c in range(CHUNKS):
            where = (pl.ds(0, by_row), slice(None), pl.ds(c * width, width))
            parts.append(pltpu.make_async_copy(tab_hbm.at[where], tab.at[where], sem.at[3 + c]))
            if c < 2:
                parts[-1].start()
    others = pl.ds(by_row, features - by_row)
    rest_copy = pltpu.make_async_copy(tab_hbm.at[others], tab.at[others], sem.at[2])
    if not by_row:
        rest_copy.start()
    for copy in copies:
        copy.wait()
    for f in range(features):
        for j in range(bag):
            shown[f * bag + j] = jnp.where(j < len_ref[pl.ds(f, 1), :], ids_ref[f, pl.ds(j, 1), :], vocab)
    if by_row:
        moves = [pltpu.make_async_copy(shown.at[n, 0], addresses[n], sem_ids.at[n]) for n in range(by_row * bag)]
        for move in moves:
            move.start()
        row_ref[pl.ds(vocab, 8), :] = jnp.zeros((8, 128), jnp.float32)
        square = [lax.broadcasted_iota(jnp.int32, (LOW, LOW), axis) for axis in range(2)]
        unit = (square[0] == square[1]).astype(jnp.float32).astype(jnp.bfloat16)
        blank = jnp.zeros((128 - by_row * embed, LOW), jnp.float32)

        def build(block, carry, first):
            start = pl.multiple_of(first + block * 2 * LOW, 2 * LOW)
            both = []
            for n in range(2):
                both += [tab[f, :, pl.ds(start + n * LOW, LOW)].astype(jnp.float32) for f in range(by_row)] + [blank]
            columns = jnp.concatenate(both, axis=0).astype(jnp.bfloat16)
            turned = lax.dot_general(unit, columns, (((1,), (1,)), ((), ())), preferred_element_type=jnp.float32)
            row_ref[pl.ds(start, LOW), :] = turned[:, :128]
            row_ref[pl.ds(start + LOW, LOW), :] = turned[:, 128:]
            return carry

        for c in range(CHUNKS):
            parts[c].wait()
            if c + 2 < CHUNKS:
                parts[c + 2].start()
            if c == CHUNKS // 2 - 1:
                rest_copy.start()
            lax.fori_loop(0, width // (2 * LOW), functools.partial(build, first=c * width), 0, unroll=8)
        for move in moves:
            move.wait()
    rest_copy.wait()
    lane = lax.broadcasted_iota(jnp.int32, (1, 128), 1)

    def other(block):
        dest = me + 1 + block
        return jnp.where(dest >= dests, dest - dests, dest)

    def lookups(group):
        eighths = row_count // 8
        row = pl.multiple_of(other(group // eighths) * row_count + group % eighths * 8, 8)
        for u in range(8):
            line = None
            for f in range(by_row):
                found = [row_ref[pl.ds(addresses[f * bag + j][row + u], 1), :] for j in range(bag)]
                total = found[0]
                for item in found[1:]:
                    total = total + item
                line = total if line is None else jnp.where(lane < embed * f, line, total)
                yield
            pooled[pl.ds(row + u, 1), :] = line

    last = (dests - 1) * row_count // 8 - 1
    tiles = samples // tile

    def step(i, carry):
        feature, t = by_row + i // tiles, i % tiles
        pl.when(t == 0)(functools.partial(arrange_low, table_low, tab, feature))
        work = (item for g in range(groups) for item in lookups(jnp.minimum(i * groups + g, last)))
        wanted = groups * 8 * by_row
        count = [0, 0]

        def between():
            count[0] += 1
            while count[1] * (bag // PAIR) * high < count[0] * wanted:
                next(work, None)
                count[1] += 1

        span = pl.ds(pl.multiple_of(t * tile, tile), tile)
        index = [shown[feature * bag + j, :, span] for j in range(bag)]
        total = pool_matched(table_low, high, index, between)
        for block in range(tile // row_count):
            piece = total[:, block * row_count : (block + 1) * row_count]
            out_ref[t * (tile // row_count) + block, feature] = piece.astype(jnp.bfloat16)
        for _ in work:
            pass
        return carry

    steps = (features - by_row) * tiles
    lax.fori_loop(0, steps, step, 0)
    if by_row:

        def rest(group, carry):
            for _ in lookups(group):
                pass
            return carry

        lax.fori_loop(min(steps * groups, last + 1), last + 1, rest, 0)
    if by_row:
        out_ref[me, pl.ds(0, by_row)] = jnp.zeros((by_row, embed, row_count), jnp.bfloat16)

        def finish(block, carry):
            dest = other(block)
            turned = pooled[pl.ds(pl.multiple_of(dest * row_count, row_count), row_count), :].T
            for f in range(by_row):
                out_ref[dest, f] = turned[f * embed : (f + 1) * embed].astype(jnp.bfloat16)
            return carry

        lax.fori_loop(0, dests - 1, finish, 0, unroll=True)


def row_features(features, embed):
    return min(128 // embed, features * 5 // 8)


def pool_features(place, table, ids, lengths, inner_size):
    features, embed, vocab = table.shape
    bag, samples = ids.shape[1], ids.shape[2]
    row_count = samples // inner_size
    tile = row_count * max(1, min(samples, 1024) // row_count)
    by_row = row_features(features, embed)
    steps = (features - by_row) * (samples // tile)
    groups = (samples - row_count) // 8 // steps if by_row else 0
    hbm = pl.BlockSpec(memory_space=pltpu.HBM)
    scratch = [
        pltpu.VMEM(ids.shape, jnp.int32),
        pltpu.VMEM(lengths.shape, jnp.int32),
        pltpu.VMEM((features * bag, 1, samples), jnp.int32),
        pltpu.VMEM(table.shape, jnp.bfloat16),
        pltpu.VMEM((vocab // LOW * embed, LOW), jnp.bfloat16),
        pltpu.SemaphoreType.DMA((3 + CHUNKS,)),
    ]
    if by_row:
        scratch += [
            pltpu.VMEM((vocab + 8, 128), jnp.float32),
            pltpu.VMEM((samples, 128), jnp.float32),
            pltpu.SemaphoreType.DMA((by_row * bag,)),
        ] + [pltpu.SMEM((samples,), jnp.int32)] * (by_row * bag)
    return pl.pallas_call(
        functools.partial(pool_kernel, by_row, tile, groups, row_count),
        out_shape=pltpu.HBM((inner_size, features, embed, row_count), jnp.bfloat16),
        in_specs=[pl.BlockSpec(memory_space=pltpu.SMEM), hbm, hbm, hbm],
        out_specs=pl.BlockSpec(memory_space=pltpu.VMEM),
        scratch_shapes=scratch,
        compiler_params=pltpu.CompilerParams(vmem_limit_bytes=32 * 2**20),
        name="pool_features",
    )(place, *(pltpu.with_memory_space_constraint(x, pltpu.HBM) for x in (ids, lengths, table)))


def own_kernel(me_ref, ids_ref, len_ref, tab_ref, out_ref, *lows):
    together, vocab = len(lows), tab_ref.shape[2]
    for f, table_low in enumerate(lows):
        arrange_low(table_low, tab_ref, f)
        length = len_ref[pl.ds(pl.program_id(0) * together + f, 1), :]
        index = [jnp.where(j < length, ids_ref[f, pl.ds(j, 1), :], vocab) for j in range(ids_ref.shape[1])]
        out_ref[f] = pool_matched(table_low, vocab // LOW, index).astype(jnp.bfloat16)


def pool_own(place, table, ids, lengths, inner_size):
    all_features, embed, vocab = table.shape
    features = row_features(all_features, embed)
    bag, samples = ids.shape[1], ids.shape[2]
    rows = samples // inner_size
    together = math.gcd(features, OWN)
    return pl.pallas_call(
        own_kernel,
        out_shape=jax.ShapeDtypeStruct((features, embed, rows), jnp.bfloat16),
        grid_spec=pltpu.PrefetchScalarGridSpec(
            num_scalar_prefetch=1,
            grid=(features // together,),
            in_specs=[
                pl.BlockSpec((together, bag, rows), lambda f, me: (f, 0, me[0])),
                pl.BlockSpec((all_features, rows), lambda f, me: (0, me[0])),
                pl.BlockSpec((together, embed, vocab), lambda f, me: (f, 0, 0)),
            ],
            out_specs=pl.BlockSpec((together, embed, rows), lambda f, me: (f, 0, 0)),
            scratch_shapes=[pltpu.VMEM((vocab // LOW * embed, LOW), jnp.bfloat16)] * together,
        ),
        compiler_params=pltpu.CompilerParams(vmem_limit_bytes=16 * 2**20),
        cost_estimate=pl.CostEstimate(
            flops=2 * features * bag * rows * vocab * embed, bytes_accessed=2 * table.size, transcendentals=0
        ),
        name="pool_own",
    )(place, *(pltpu.with_memory_space_constraint(x, pltpu.HBM) for x in (ids, lengths, table)))


def early_kernel(known, tower_ref, other_ref, own_hbm, far_hbm, own_bias_ref, far_bias_ref, gate_ref, *refs):
    early_ref, gate_early_ref, late_ref, gate_late_ref, weights, sem = refs
    tower = tower_ref[0]
    half, experts_in, columns = own_hbm.shape[0], weights.shape[1], weights.shape[2]
    span = pl.ds(pl.multiple_of(tower * columns, columns), columns)
    copies = []
    for n, (source, place) in enumerate([(own_hbm, tower), (far_hbm, 1 - tower)]):
        for e in range(half):
            copies.append(
                pltpu.make_async_copy(source.at[e, :, span], weights.at[place * half + e], sem.at[n * half + e])
            )
            copies[-1].start()
    tasks, experts, depth = gate_ref.shape
    gates = gate_ref[...].astype(jnp.float32).reshape(tasks * experts, depth).astype(jnp.bfloat16)
    gate_early_ref[...] = lax.dot_general(
        other_ref[...], gates[:, :known], (((1,), (1,)), ((), ())), preferred_element_type=jnp.float32
    )
    gate_late_ref[...] = gates[:, known:]
    for n, (bias, place) in enumerate([(own_bias_ref, tower), (far_bias_ref, 1 - tower)]):
        for e in range(half):
            copies[n * half + e].wait()
            at = place * half + e
            found = jnp.dot(other_ref[...], weights[at, pl.ds(0, known), :], preferred_element_type=jnp.float32)
            early_ref[at] = found + bias[pl.ds(e, 1), span]
            late_ref[at] = weights[at, pl.ds(known, experts_in - known), :]


def early_part(tower, other, own_w, far_w, own_b, far_b, gates):
    half, depth, hidden = own_w.shape
    rows, known = other.shape
    columns = hidden // 2
    vmem, hbm = pl.BlockSpec(memory_space=pltpu.VMEM), pl.BlockSpec(memory_space=pltpu.HBM)
    count = gates.shape[0] * gates.shape[1]
    far = lambda x: pltpu.with_memory_space_constraint(x, pltpu.HBM)
    return pl.pallas_call(
        functools.partial(early_kernel, known),
        out_shape=(
            jax.ShapeDtypeStruct((2 * half, rows, columns), jnp.float32),
            jax.ShapeDtypeStruct((rows, count), jnp.float32),
            jax.ShapeDtypeStruct((2 * half, depth - known, columns), jnp.bfloat16),
            jax.ShapeDtypeStruct((count, depth - known), jnp.bfloat16),
        ),
        in_specs=[pl.BlockSpec(memory_space=pltpu.SMEM), vmem, hbm, hbm, vmem, vmem, vmem],
        out_specs=(vmem,) * 4,
        scratch_shapes=[pltpu.VMEM((2 * half, depth, columns), jnp.bfloat16), pltpu.SemaphoreType.DMA((2 * half,))],
        compiler_params=pltpu.CompilerParams(vmem_limit_bytes=16 * 2**20),
        cost_estimate=pl.CostEstimate(
            flops=4 * half * rows * known * columns,
            bytes_accessed=4 * half * depth * columns,
            transcendentals=0,
        ),
        name="early_part",
    )(tower, other, far(own_w), far_w, own_b, far_b, gates)


def cross_kernel(each, by_row, me_ref, slot_ref, rec_ref, own_ref, w_hbm, bias_ref, comp_ref, comp_bias_ref, *refs):
    out_ref, first_t, first, w_ref, sums, sem = refs
    slots, embed, rows = rec_ref.shape
    width, blocks = w_ref.shape[1], sem.shape[0]
    step = width // blocks
    spans = [pl.ds(n * step, step) for n in range(blocks)]
    copies = [pltpu.make_async_copy(w_hbm.at[span], w_ref.at[span], sem.at[n]) for n, span in enumerate(spans)]
    for copy in copies:
        copy.start()
    for f in range(slots):
        first_t[slot_ref[f]] = rec_ref[f].astype(jnp.float32)
    for f in range(by_row):
        first_t[slot_ref[me_ref[0] * each + f]] = own_ref[f].astype(jnp.float32)
    first[...] = first_t[...].reshape(width, rows).T.astype(jnp.bfloat16)
    crossed = bias_ref[...]
    for n, span in enumerate(spans):
        copies[n].wait()
        crossed = crossed + jnp.dot(first[:, span], w_ref[span, :], preferred_element_type=jnp.float32)
        if n + 1 < blocks:
            sums[...] = crossed
            crossed = sums[...]
    total = jnp.zeros((rows, comp_ref.shape[0]), jnp.float32) + comp_bias_ref[...]
    for n, span in enumerate(spans):
        base = first[:, span].astype(jnp.float32)
        second = (base * crossed[:, n * step : (n + 1) * step] + base).astype(jnp.bfloat16)
        total = total + lax.dot_general(
            second, comp_ref[:, span], (((1,), (1,)), ((), ())), preferred_element_type=jnp.float32
        )
    out_ref[...] = total.astype(jnp.bfloat16)


def cross_and_compress(place, slots, received, own, by_row, each, cross_w, cross_b, comp_w, comp_b):
    slot_total, embed, rows = received.shape
    width = cross_w.shape[0]
    vmem, smem = pl.BlockSpec(memory_space=pltpu.VMEM), pl.BlockSpec(memory_space=pltpu.SMEM)
    return pl.pallas_call(
        functools.partial(cross_kernel, each, by_row),
        out_shape=jax.ShapeDtypeStruct((rows, comp_w.shape[1]), jnp.bfloat16),
        in_specs=[smem, smem, vmem, vmem, pl.BlockSpec(memory_space=pltpu.HBM), vmem, vmem, vmem],
        out_specs=vmem,
        scratch_shapes=[
            pltpu.VMEM((slot_total, embed, rows), jnp.float32),
            pltpu.VMEM((rows, width), jnp.bfloat16),
            pltpu.VMEM(cross_w.shape, jnp.bfloat16),
            pltpu.VMEM((rows, width), jnp.float32),
            pltpu.SemaphoreType.DMA((width // 256,)),
        ],
        compiler_params=pltpu.CompilerParams(vmem_limit_bytes=16 * 2**20),
        name="cross_and_compress",
    )(place, slots, received, own, pltpu.with_memory_space_constraint(cross_w, pltpu.HBM), cross_b, comp_w.T, comp_b)


def mix_kernel(tower_ref, early_ref, late_ref, gate_early_ref, gate_late_ref, own_ref, far_ref, out_ref, hidden_ref, lines_ref):
    experts, rows, columns = early_ref.shape
    tasks = gate_early_ref.shape[1] // experts
    own, far = own_ref[...], far_ref[...]
    lead = tower_ref[0] == 0
    squeezed = jnp.concatenate([jnp.where(lead, own, far), jnp.where(lead, far, own)], axis=1)
    logits = gate_early_ref[...] + lax.dot_general(
        squeezed, gate_late_ref[...], (((1,), (1,)), ((), ())), preferred_element_type=jnp.float32
    )
    weights = jnp.exp(logits)
    probs = []
    for k in range(tasks):
        mine = weights[:, k * experts : (k + 1) * experts]
        probs.append(mine / jnp.sum(mine, axis=1, keepdims=True))
    for e in range(experts):
        hidden = early_ref[e] + jnp.dot(squeezed, late_ref[e], preferred_element_type=jnp.float32)
        hidden_ref[e] = jnp.maximum(hidden, 0.0).astype(jnp.bfloat16).astype(jnp.float32)
    step = math.gcd(rows, 32)
    for first in range(0, rows, step):
        totals = [0.0] * tasks
        for e in range(experts):
            hidden = hidden_ref[e, pl.ds(first, step), :]
            for k in range(tasks):
                totals[k] = totals[k] + probs[k][first : first + step, e : e + 1] * hidden
        for c in range(columns // 128):
            for k in range(tasks):
                lines_ref[c, pl.ds(first * tasks + k, step, stride=tasks), :] = totals[k][:, c * 128 : (c + 1) * 128]
            lines = lines_ref[c, pl.ds(first * tasks, step * tasks), :].reshape(step, tasks, 128)
            out_ref[pl.ds(first, step), :, pl.ds(c * 128, 128)] = lines.astype(jnp.bfloat16)


def mix_experts(tower, early, late, gate_early, gate_late, own, far):
    experts, rows, columns = early.shape
    tasks = gate_early.shape[1] // experts
    vmem = pl.BlockSpec(memory_space=pltpu.VMEM)
    return pl.pallas_call(
        mix_kernel,
        out_shape=jax.ShapeDtypeStruct((rows, tasks, columns), jnp.bfloat16),
        in_specs=[pl.BlockSpec(memory_space=pltpu.SMEM)] + [vmem] * 6,
        out_specs=vmem,
        scratch_shapes=[
            pltpu.VMEM((experts, rows, columns), jnp.float32),
            pltpu.VMEM((columns // 128, rows * tasks, 128), jnp.float32),
        ],
        compiler_params=pltpu.CompilerParams(vmem_limit_bytes=16 * 2**20),
        name="mix_experts",
    )(tower, early, late, gate_early, gate_late, own, far)


def on_device(
    ids,
    bag_len,
    slot_of_feature,
    tables,
    cross_w,
    cross_b,
    comp_w,
    comp_b,
    other_towers,
    expert_w,
    expert_b,
    gate_w,
):
    inner_size = lax.axis_size("inner")
    tower_size = lax.axis_size("tower")
    tower = lax.axis_index("tower")
    swap = [(n, (n + 1) % tower_size) for n in range(tower_size)]

    far_w = lax.ppermute(expert_w, "tower", swap)
    far_b = lax.ppermute(expert_b, "tower", swap)

    here = lax.axis_index("inner").reshape(1)
    tables_t, ids_t = jnp.transpose(tables[0], (0, 2, 1)), jnp.transpose(ids[0], (0, 2, 1))
    pooled = pool_features(here, tables_t, ids_t, bag_len[0], inner_size)
    dests, features, embed, rows = pooled.shape
    pooled = pooled.reshape(dests, features * embed, rows)
    received = lax.all_to_all(pooled, "inner", split_axis=0, concat_axis=0, tiled=True)
    received = received.reshape(dests * features, embed, rows)

    by_row = row_features(features, embed)
    own = pool_own(here, tables_t, ids_t, bag_len[0], inner_size) if by_row else received[:1]
    place = tower.reshape(1)
    gates = jnp.transpose(gate_w, (1, 2, 0))
    early = early_part(place, other_towers, expert_w, far_w, expert_b, far_b, gates)
    hidden_early, gate_early, late_w, gate_late = early
    received, own, hidden_early = lax.optimization_barrier((received, own, hidden_early))

    squeezed = cross_and_compress(here, slot_of_feature[0], received, own, by_row, features, cross_w[0], cross_b, comp_w[0], comp_b)
    opposite = lax.ppermute(squeezed, "tower", swap)
    return mix_experts(place, hidden_early, late_w, gate_early, gate_late, squeezed, opposite)


def solution(mesh):
    return jax.shard_map(
        on_device,
        mesh=mesh,
        in_specs=(
            P("tower", "inner", "groups", None),
            P("tower", "inner", "groups"),
            P("tower", None),
            P("tower", "inner", None, None),
            P("tower", None, None),
            P("tower", None),
            P("tower", None, None),
            P("tower", None),
            P(("groups", "inner"), None),
            P("tower", None, None),
            P("tower", None),
            P(),
        ),
        out_specs=P(("groups", "inner"), None, "tower"),
        check_vma=False,
    )
```
